32 devices in a mesh: expert: 16 (over z, y, x), tensor: 2 (over core).
Axes of the slice: x: 2, y: 2, z: 4, core: 2. Of those that a mesh axis runs over, the one named last changes fastest.
Arguments:
- tokens: bfloat16 [768, 4096], P('expert', 'tensor'), may hold values from -6 to 6
- cotangent: bfloat16 [768, 4096], P('expert', 'tensor'), may hold values from -6 to 6
- expert_ids: int32 [768, 8], P('expert'), may hold values from 0 to 15, all different within a row; in each aligned block of 48 rows (0 to 47, 48 to 95, ...) at most 32 rows name the same one
- gate_values: float32 [768, 8], P('expert'), may hold values from 0.05 to 1
- w_gate: bfloat16 [16, 768, 4096], P('expert', 'tensor'), may hold values from -0.09375 to 0.09375
- w_up: bfloat16 [16, 768, 4096], P('expert', 'tensor'), may hold values from -0.09375 to 0.09375
- w_down: bfloat16 [16, 768, 4096], P('expert', 'tensor'), may hold values from -0.21875 to 0.21875
Outputs:
- grad_tokens: bfloat16 [768, 4096], P('expert', 'tensor')
- grad_gate: bfloat16 [16, 768, 4096], P('expert', 'tensor')
- grad_up: bfloat16 [16, 768, 4096], P('expert', 'tensor')
- grad_down: bfloat16 [16, 768, 4096], P('expert', 'tensor')
The draws below stay inside these ranges and needn't reach their ends.
Inputs may be any that keep to these rules, and one draw needn't show every extreme that they name: `expert_ids`: each row names 8 different experts. Among the 48 tokens of one index of the expert axis no expert is named more than 32 times, and in every draw some expert is named exactly 32 times there.
All inputs are finite; a program needn't handle non-finite values.
Results may differ from the reference program's by a relative error of at most 0.019.
Values may be sent and summed in bfloat16 or wider, within the bound.
A program may use at most 64 MiB of HBM per device.

```python
import math
import jax
import jax.numpy as jnp
import numpy as np
from jax import lax

D = 4096
HID = 768
TOP = 8
TOK_DEV = 48
EXPERTS = 16
CAP = 32
TOKENS = 768
N_EXPERT = 16
N_TENSOR = 2


def steps_of(rng, extent, pieces, least, high):
    gain = 1.0
    for dim, shards_of in pieces:
        heights = jax.random.uniform(jax.random.fold_in(jax.random.fold_in(rng, 6), dim), (shards_of,), jnp.float32, least / len(pieces), high / len(pieces))
        gain = gain * jnp.repeat(jnp.exp(heights), extent[dim] // shards_of).reshape((-1,) + (1,) * (len(extent) - 1 - dim))
    return gain


def shared_out(rng, own, number, rows, count, top, reach, slope):
    sequence = jax.random.permutation(rng, count)
    heavy_load, common = load_shares(count, rows * top, reach, slope, True), load_shares(count, rows * top, reach, slope, False)
    places = jnp.arange(count)

    def named(lengths, turn):
        used = int((lengths > 0).sum())
        fixed = max(1, used // 4)
        moved = fixed + (places - fixed + turn * (used - fixed)) % max(1, count - fixed)
        return jnp.zeros((count,), jnp.int32).at[sequence[jnp.where(places < fixed, places, moved)]].set(jnp.asarray(lengths, jnp.int32))

    lengths = jnp.where(number % 4 == 0, named(heavy_load, number // 4), named(common, number - number // 4 - 1))
    mixed = jax.random.permutation(jax.random.fold_in(own, 3), count)
    donor, receiver = mixed[0:count // 2 * 2:2], mixed[1:count // 2 * 2:2]
    room = jnp.minimum(lengths[donor] - 1, reach - lengths[receiver]) // 2
    room = jnp.where((donor == sequence[0]) | (receiver == sequence[0]) | (lengths[receiver] == 0), 0, jnp.maximum(room, 0))
    moved = jax.random.randint(jax.random.fold_in(own, 4), (count // 2,), 0, 1 << 20) % (room + 1)
    lengths = lengths.at[donor].add(-moved).at[receiver].add(moved)
    members = jnp.searchsorted(jnp.cumsum(lengths), jnp.arange(rows * top), side="right").astype(jnp.int32)
    listing = members.reshape(top, rows).T
    listing = listing[jax.random.permutation(jax.random.fold_in(own, 1), rows)]
    turn = jax.random.randint(jax.random.fold_in(own, 2), (rows, 1), 0, top)
    return jnp.take_along_axis(listing, (jnp.arange(top)[None, :] + turn) % top, axis=1)


def load_shares(count, total, reach, lean, full):
    loads = [(1 << 20) // math.isqrt(rank ** lean) + 1 for rank in range(1, count + 1)]
    largest = reach if full else min(reach, max(-(-total // count), total * loads[0] // sum(loads)))
    least = 1 if total - largest >= count - 1 else 0
    counts, surplus = [largest] + [least] * (count - 1), total - largest - least * (count - 1)
    while surplus > 0:
        free = [i for i in range(1, count) if counts[i] < largest] or [i for i in range(1, count) if counts[i] < reach]
        pool, remaining = sum([loads[i] for i in free]), surplus
        for i in free:
            more = min(reach - counts[i], max(1, remaining * loads[i] // pool), surplus)
            counts[i] = counts[i] + more
            surplus = surplus - more
    return np.array(counts)


def scatter_about(rng, extent, scale, bound, split=(), held_as=jnp.bfloat16):
    entries = jax.random.normal(rng, extent, jnp.float32) * scale
    if len(split) > 0:
        entries = steps_of(rng, extent, split, -0.22, 0.18) * entries
    return jnp.clip(entries, min=-bound, max=bound).astype(held_as)


def setup_inputs(seed: int = 0) -> dict:
    arg_keys = jax.random.split(jax.random.key(seed), 8)
    tokens = scatter_about(arg_keys[0], (TOKENS, D), 1.0, 6.0, ((0, 16), (1, 2)))
    cotangent = scatter_about(arg_keys[1], (TOKENS, D), 1.0, 6.0, ((0, 16), (1, 2)))
    expert_ids_keys = jax.random.split(jax.random.fold_in(arg_keys[2], 1), TOKENS // TOK_DEV)
    expert_ids_turns = jax.random.permutation(jax.random.fold_in(arg_keys[2], 3), TOKENS // TOK_DEV)
    expert_ids = jax.vmap(lambda own, number: shared_out(jax.random.fold_in(arg_keys[2], 2), own, number, TOK_DEV, EXPERTS, TOP, CAP, 2))(expert_ids_keys, expert_ids_turns).reshape((TOKENS, TOP))
    gate_values = jnp.clip(jnp.exp(math.log(1.0) - 2.9957323 * jax.random.uniform(arg_keys[3], (TOKENS, TOP), jnp.float32) ** steps_of(arg_keys[3], (TOKENS, TOP), ((0, 16),), -0.2, 0.2)), 0.05, 1.0)
    w_gate = scatter_about(arg_keys[4], (EXPERTS, HID, D), D ** -0.5, 0.09375, ((0, 16), (1, 2)))
    w_up = scatter_about(arg_keys[5], (EXPERTS, HID, D), D ** -0.5, 0.09375, ((0, 16), (1, 2)))
    w_down = scatter_about(arg_keys[6], (EXPERTS, HID, D), HID ** -0.5, 0.21875, ((0, 16), (1, 2)))
    return dict(tokens=tokens, cotangent=cotangent, expert_ids=expert_ids, gate_values=gate_values, w_gate=w_gate, w_up=w_up, w_down=w_down)


def reference(tokens, cotangent, expert_ids, gate_values, w_gate, w_up, w_down):
    per_block = TOK_DEV * TOP
    flat_ids = expert_ids.reshape(N_EXPERT, per_block)
    onehot = (flat_ids[:, :, None] == jnp.arange(EXPERTS, dtype=jnp.int32)[None, None, :]).astype(jnp.int32)
    before = jnp.cumsum(onehot, axis=1) - onehot
    slot_pos = jnp.sum(before * onehot, axis=2).astype(jnp.int32)
    token_index = (jnp.arange(TOKENS, dtype=jnp.int32)[:, None] + jnp.zeros((1, TOP), jnp.int32)).reshape(N_EXPERT, per_block)
    source = jnp.arange(N_EXPERT, dtype=jnp.int32)[:, None] + jnp.zeros((1, per_block), jnp.int32)
    slot_owner = jnp.full((EXPERTS, N_EXPERT, CAP), -1, jnp.int32).at[flat_ids, source, slot_pos].set(token_index)
    slot_gate = jnp.zeros((EXPERTS, N_EXPERT, CAP), jnp.float32).at[flat_ids, source, slot_pos].set(gate_values.reshape(N_EXPERT, per_block))
    row_count = N_EXPERT * CAP

    def one_expert(accumulated, per_expert):
        owner_e, gate_e, gate_mat, up_mat, down_mat = per_expert
        occupied = (owner_e >= 0).reshape(-1)
        row_index = jnp.maximum(owner_e, 0).reshape(-1).astype(jnp.int32)
        rows_x = jnp.where(occupied[:, None], tokens[row_index], jnp.zeros((), jnp.bfloat16))
        scaled = gate_e.reshape(-1)[:, None] * cotangent[row_index].astype(jnp.float32)
        rows_d = jnp.where(occupied[:, None], scaled, jnp.zeros((), jnp.float32)).astype(jnp.bfloat16)
        gate_pre = jnp.dot(rows_x, gate_mat.T, preferred_element_type=jnp.float32)
        up_pre = jnp.dot(rows_x, up_mat.T, preferred_element_type=jnp.float32)
        sigmoid = jax.nn.sigmoid(gate_pre)
        active = gate_pre * sigmoid
        hidden = (active * up_pre).astype(jnp.bfloat16)
        hidden_grad = jnp.dot(rows_d, down_mat.T, preferred_element_type=jnp.float32)
        up_grad = (hidden_grad * active).astype(jnp.bfloat16)
        gate_grad = (hidden_grad * up_pre * sigmoid * (1.0 + gate_pre * (1.0 - sigmoid))).astype(jnp.bfloat16)
        grad_g = jnp.dot(gate_grad.T, rows_x, preferred_element_type=jnp.float32).astype(jnp.bfloat16)
        grad_u = jnp.dot(up_grad.T, rows_x, preferred_element_type=jnp.float32).astype(jnp.bfloat16)
        grad_d = jnp.dot(hidden.T, rows_d, preferred_element_type=jnp.float32).astype(jnp.bfloat16)
        part_sums = jnp.einsum('rph,phd->prd', gate_grad.reshape(row_count, N_TENSOR, -1).astype(jnp.float32), gate_mat.reshape(N_TENSOR, -1, D).astype(jnp.float32))
        part_sums = part_sums + jnp.einsum('rph,phd->prd', up_grad.reshape(row_count, N_TENSOR, -1).astype(jnp.float32), up_mat.reshape(N_TENSOR, -1, D).astype(jnp.float32))
        rounded = lax.optimization_barrier(part_sums.astype(jnp.bfloat16))
        row_grad = jnp.sum(rounded.astype(jnp.float32), axis=0).astype(jnp.bfloat16)
        addend = jnp.where(occupied[:, None], row_grad.astype(jnp.float32), jnp.zeros((), jnp.float32))
        accumulated = accumulated.at[row_index].add(addend)
        return accumulated, (grad_g, grad_u, grad_d)

    accumulated, grads = lax.scan(one_expert, jnp.zeros((TOKENS, D), jnp.float32), (slot_owner, slot_gate, w_gate, w_up, w_down))
    return accumulated.astype(jnp.bfloat16), grads[0], grads[1], grads[2]
```

```python
import jax
import jax.numpy as jnp
from jax import lax
from jax.experimental import pallas as pl
from jax.experimental.pallas import tpu as pltpu
from jax.sharding import PartitionSpec as P

TOP = 8
MESH = pl.DeviceIdType.MESH


def expert_backward(rows_x, rows_d, w_gate, w_up, w_down):
    gate_pre = jnp.einsum("secd,ehd->sech", rows_x, w_gate, preferred_element_type=jnp.float32)
    up_pre = jnp.einsum("secd,ehd->sech", rows_x, w_up, preferred_element_type=jnp.float32)
    sigmoid = jax.nn.sigmoid(gate_pre)
    active = gate_pre * sigmoid
    hidden = (active * up_pre).astype(jnp.bfloat16)
    hidden_grad = jnp.einsum("secd,ehd->sech", rows_d, w_down, preferred_element_type=jnp.float32)
    up_grad = (hidden_grad * active).astype(jnp.bfloat16)
    gate_grad = (hidden_grad * up_pre * sigmoid * (1.0 + gate_pre * (1.0 - sigmoid))).astype(
        jnp.bfloat16
    )
    grad_gate = jnp.einsum(
        "sech,secd->ehd", gate_grad, rows_x, preferred_element_type=jnp.float32
    ).astype(jnp.bfloat16)
    grad_up = jnp.einsum(
        "sech,secd->ehd", up_grad, rows_x, preferred_element_type=jnp.float32
    ).astype(jnp.bfloat16)
    grad_down = jnp.einsum(
        "sech,secd->ehd", hidden, rows_d, preferred_element_type=jnp.float32
    ).astype(jnp.bfloat16)
    partial_value = jnp.einsum(
        "sech,ehd->secd", gate_grad, w_gate, preferred_element_type=jnp.float32
    )
    partial_value = partial_value + jnp.einsum(
        "sech,ehd->secd", up_grad, w_up, preferred_element_type=jnp.float32
    )
    return (partial_value, grad_gate, grad_up, grad_down)


def on_device(tokens, cotangent, expert_ids, gate_values, w_gate, w_up, w_down):
    tok_count = expert_ids.shape[0]
    local_count = w_gate.shape[0]
    groups = lax.axis_size("expert")
    experts = local_count * groups
    capacity = 4 * tok_count * TOP // (3 * experts)
    feat_width = tokens.shape[1]
    flat_ids = expert_ids.reshape(-1)
    onehot = (flat_ids[:, None] == jnp.arange(experts, dtype=jnp.int32)[None, :]).astype(jnp.int32)
    before = jnp.cumsum(onehot, axis=0) - onehot
    slot_pos = jnp.sum(before * onehot, axis=1)
    target = flat_ids * capacity + slot_pos
    matches = (target[None, :] == jnp.arange(experts * capacity, dtype=jnp.int32)[:, None]).reshape(
        experts * capacity, tok_count, TOP
    )
    by_token = jnp.any(matches, axis=2)
    occupied = jnp.any(by_token, axis=1)
    token_iota = jnp.arange(tok_count, dtype=jnp.int32)
    owner = jnp.sum(jnp.where(by_token, token_iota[None, :], 0), axis=1)
    slot_weight = jnp.sum(jnp.sum(jnp.where(matches, gate_values[None, :, :], 0.0), axis=2), axis=1)
    full_x, full_d = (
        lax.all_gather(tokens, "tensor", axis=1, tiled=True),
        lax.all_gather(cotangent, "tensor", axis=1, tiled=True),
    )
    sent_x = jnp.where(occupied[:, None], full_x[owner], jnp.zeros((), jnp.bfloat16))
    sent_d = (slot_weight[:, None] * full_d[owner].astype(jnp.float32)).astype(jnp.bfloat16)
    buffer_shape = (groups, local_count, capacity, full_x.shape[1])
    sent_x, sent_d = (sent_x.reshape(buffer_shape), sent_d.reshape(buffer_shape))
    rows_x, rows_d = (
        lax.all_to_all(sent_x, "expert", split_axis=0, concat_axis=0, tiled=True),
        lax.all_to_all(sent_d, "expert", split_axis=0, concat_axis=0, tiled=True),
    )
    partial_value, grad_gate, grad_up, grad_down = expert_backward(
        rows_x, rows_d, w_gate, w_up, w_down
    )
    summed = lax.psum(partial_value.astype(jnp.bfloat16), "tensor").astype(jnp.float32)
    returned = lax.dynamic_slice_in_dim(
        summed, lax.axis_index("tensor") * feat_width, feat_width, 3
    ).astype(jnp.bfloat16)
    arrived = lax.all_to_all(returned, "expert", split_axis=0, concat_axis=0, tiled=True).reshape(
        experts * capacity, feat_width
    )
    masked = jnp.where(occupied[:, None], arrived.astype(jnp.float32), jnp.zeros((), jnp.float32))
    grad_tokens = jax.ops.segment_sum(masked, owner, num_segments=tok_count).astype(jnp.bfloat16)
    return (grad_tokens, grad_gate, grad_up, grad_down)


def merge_kernel(
    tok_ref, cot_ref, gate_ref, wg_ref, wu_ref, wd_ref,
    out_ref, gg_ref, gu_ref, gd_ref,
    xs, ds_, wgu, wd, pre, hgrad, act, hid, act_t, hid_t, part, sib_out, sib_in, from_last, from_z, from_first,
    stage, load_sem, send, recv, sib_send, sib_recv, last_send, last_recv, z_send, z_recv, first_send, first_recv, out_sem,
):
    rows = tok_ref.shape[0]
    half = tok_ref.shape[1]
    hidden = wg_ref.shape[1]
    plane_rows = 4 * rows
    f32 = jnp.float32
    e, c = lax.axis_index("expert"), lax.axis_index("tensor")
    x, y, z = e % 2, (e // 2) % 2, e // 4
    a, b = x + c * (y - x), y + c * (x - y)

    def index(aa, bb, zz):
        return zz * 4 + aa * (1 + c) + bb * (2 - c)

    def where(expert, core):
        return dict(device_id={"expert": expert, "tensor": core}, device_id_type=MESH)

    first, last = index(1 - a, b, z), index(a, 1 - b, z)
    up, down = e + 4, e - 4
    bufs = (xs, ds_)

    loads = []
    for t, ref in enumerate((tok_ref, cot_ref)):
        loads.append(pltpu.make_async_copy(
            ref, bufs[t].at[c, pl.ds(pl.multiple_of(e * rows, 16), rows), pl.ds(0, half)], load_sem.at[t]))
    n = 2
    weights = []
    for h in range(2):
        cols = pl.ds(h * half, half)
        weights.append(pltpu.make_async_copy(wg_ref.at[0, :, cols], wgu.at[h, pl.ds(0, hidden)], load_sem.at[n]))
        weights.append(pltpu.make_async_copy(wu_ref.at[0, :, cols], wgu.at[h, pl.ds(hidden, hidden)], load_sem.at[n + 1]))
        weights.append(pltpu.make_async_copy(wd_ref.at[0, :, cols], wd.at[h], load_sem.at[n + 2]))
        n += 3
    for copy in loads + weights:
        copy.start()
    ds_[c, pl.ds(pl.multiple_of(e * rows, 16), rows), half:] = gate_ref[...]

    barrier = pltpu.get_barrier_semaphore()
    pl.semaphore_signal(barrier, inc=1, **where(first, c))
    pl.semaphore_signal(barrier, inc=1, **where(last, c))
    pl.semaphore_signal(barrier, inc=1, **where(e, 1 - c))

    @pl.when(z < 3)
    def _():
        pl.semaphore_signal(barrier, inc=1, **where(up, c))

    @pl.when(z > 0)
    def _():
        pl.semaphore_signal(barrier, inc=1, **where(down, c))

    pl.semaphore_wait(barrier, 4 + (z + 1) // 2 % 2)
    for copy in loads:
        copy.wait()

    def gather_copy(t, kind, blk, core):
        target = (first, up, down, last, e)[kind]
        view = bufs[t].at[core, pl.ds(pl.multiple_of(blk * rows, 16), rows)]
        return pltpu.make_async_remote_copy(
            src_ref=view, dst_ref=view, send_sem=send.at[t, kind, blk], recv_sem=recv.at[t, kind // 4, blk],
            **where(target, 1 - c if kind == 4 else c))

    def arrive(t, blk):
        gather_copy(t, 0, blk, c).wait_recv()

    def pass_on(t, blk, kinds):
        for kind in kinds:
            copy = gather_copy(t, kind, blk, c)
            if kind == 1:
                pl.when(z < 3)(copy.start)
            elif kind == 2:
                pl.when(z > 0)(copy.start)
            else:
                copy.start()

    def own(t):
        pass_on(t, e, (0, 1, 2, 3, 4))

    def first_step(t):
        blk = index(1 - a, b, z)
        arrive(t, blk)
        pass_on(t, blk, (1, 2, 3, 4))

    def z_step(t, k):
        for aa in (a, 1 - a):
            @pl.when(z >= k)
            def _():
                blk = index(aa, b, z - k)
                arrive(t, blk)
                pass_on(t, blk, (1, 3, 4))

            @pl.when(z + k <= 3)
            def _():
                blk = index(aa, b, z + k)
                arrive(t, blk)
                pass_on(t, blk, (2, 3, 4))

    def last_step(t, k):
        for aa in (a, 1 - a):
            if k == 0:
                arrive(t, index(aa, 1 - b, z))
                pass_on(t, index(aa, 1 - b, z), (4,))
                continue

            @pl.when(z >= k)
            def _():
                arrive(t, index(aa, 1 - b, z - k))
                pass_on(t, index(aa, 1 - b, z - k), (4,))

            @pl.when(z + k <= 3)
            def _():
                arrive(t, index(aa, 1 - b, z + k))
                pass_on(t, index(aa, 1 - b, z + k), (4,))

    def sibling_step(t):
        @pl.loop(0, 16)
        def _(blk):
            gather_copy(t, 4, blk, 1 - c).wait_recv()

    def gather_sent(t):
        def wait(blk, kinds):
            for kind in kinds:
                copy = gather_copy(t, kind, blk, c)
                if kind == 1:
                    pl.when(z < 3)(copy.wait_send)
                elif kind == 2:
                    pl.when(z > 0)(copy.wait_send)
                else:
                    copy.wait_send()

        wait(e, (0, 1, 2, 3, 4))
        wait(index(1 - a, b, z), (1, 2, 3, 4))
        for k in range(1, 4):
            for aa in (a, 1 - a):
                pl.when(z >= k)(lambda: wait(index(aa, b, z - k), (1, 3, 4)))
                pl.when(z + k <= 3)(lambda: wait(index(aa, b, z + k), (2, 3, 4)))

        @pl.loop(0, 4)
        def _(zz):
            for aa in range(2):
                gather_copy(t, 4, index(aa, 1 - b, zz), c).wait_send()

    def plane_view(zz):
        return pl.ds(pl.multiple_of(zz * plane_rows, 16), plane_rows)

    contract_last = (((1,), (1,)), ((), ()))

    def forward(zz):
        at = plane_view(zz)

        @pl.loop(0, 2 * hidden // 256)
        def _(j):
            cols = pl.ds(pl.multiple_of(j * 256, 256), 256)
            pre[at, cols] = lax.dot_general(
                xs[0, at, :], wgu[0, cols, :], contract_last, preferred_element_type=f32
            ) + lax.dot_general(xs[1, at, :], wgu[1, cols, :], contract_last, preferred_element_type=f32)

    own(0)
    first_step(0)
    z_step(0, 1)
    own(1)
    last_step(0, 0)
    z_step(0, 2)
    last_step(0, 1)
    z_step(0, 3)
    first_step(1)
    last_step(0, 2)
    z_step(1, 1)
    last_step(0, 3)
    for copy in weights:
        copy.wait()
    last_step(1, 0)
    sibling_step(0)
    forward(0)
    z_step(1, 2)
    forward(1)
    last_step(1, 1)
    z_step(1, 3)
    forward(2)
    last_step(1, 2)
    forward(3)
    last_step(1, 3)
    sibling_step(1)

    def plane_of(q):
        swapped = (0, 1, 3, 2)[q]
        turn = q + ((z + 1) // 2 % 2) * (swapped - q)
        high = z // 2
        return high * turn + (1 - high) * (3 - turn)

    def sibling_copy(zz):
        at = plane_view(zz)
        return pltpu.make_async_remote_copy(
            src_ref=sib_out.at[at], dst_ref=sib_in.at[at], send_sem=sib_send.at[zz], recv_sem=sib_recv.at[zz],
            **where(e, 1 - c))

    def backward(zz):
        at = plane_view(zz)
        hgrad[...] = lax.dot_general(
            ds_[0, at, pl.ds(0, half)], wd[0], contract_last, preferred_element_type=f32
        ) + lax.dot_general(ds_[1, at, pl.ds(0, half)], wd[1], contract_last, preferred_element_type=f32)

        @pl.loop(0, 4)
        def _(i):
            here = pl.ds(pl.multiple_of(zz * plane_rows + i * rows, 16), rows)
            lane = lax.broadcasted_iota(jnp.int32, (rows, 128), 1)
            pieces = ds_[0, here, pl.ds(half, 128)].astype(f32)
            weight = jnp.sum(jnp.where(jnp.bitwise_and(lane, 15) == e, pieces, 0.0), axis=1, keepdims=True)
            gate_pre, up_pre = pre[here, pl.ds(0, hidden)], pre[here, pl.ds(hidden, hidden)]
            sigmoid = 1.0 / (1.0 + jnp.exp(-gate_pre))
            active = gate_pre * sigmoid
            grad = hgrad[pl.ds(pl.multiple_of(i * rows, 16), rows), :] * weight
            hid[here, :] = (active * up_pre * weight).astype(jnp.bfloat16)
            act[here, pl.ds(hidden, hidden)] = (grad * active).astype(jnp.bfloat16)
            act[here, pl.ds(0, hidden)] = (
                grad * up_pre * sigmoid * (1.0 + gate_pre * (1.0 - sigmoid))).astype(jnp.bfloat16)

        for side, dest in ((1 - c, sib_out), (c, part)):
            @pl.loop(0, half // 512)
            def _(j):
                cols = pl.ds(pl.multiple_of(j * 512, 512), 512)
                dest[at, cols] = jnp.dot(
                    act[at, :], wgu[side, :, cols], preferred_element_type=f32).astype(jnp.bfloat16)
            if dest is sib_out:
                sibling_copy(zz).start()

    def add_rows(dest, start, count, sources):
        @pl.loop(0, count // 16)
        def _(i):
            here = pl.ds(pl.multiple_of(start + i * 16, 16), 16)
            total = dest[here, :].astype(f32)
            for ref, lead, offset in sources:
                there = pl.ds(pl.multiple_of(offset + i * 16, 16), 16)
                total = total + (ref[there, :] if lead is None else ref[lead, there, :]).astype(f32)
            dest[here, :] = total.astype(jnp.bfloat16)

    def block(blk):
        return pl.ds(pl.multiple_of(blk * rows, 16), rows)

    def last_copy(zz, aa):
        slot = zz * 2 + aa
        return pltpu.make_async_remote_copy(
            src_ref=part.at[block(index(aa, 1 - b, zz))], dst_ref=from_last.at[slot],
            send_sem=last_send.at[slot], recv_sem=last_recv.at[slot], **where(last, c))

    def z_copy(way, zz, aa):
        slot = way * 8 + zz * 2 + aa
        return pltpu.make_async_remote_copy(
            src_ref=part.at[block(index(aa, b, zz))], dst_ref=from_z.at[slot],
            send_sem=z_send.at[slot], recv_sem=z_recv.at[slot], **where(down if way else up, c))

    def reduce_last(zz):
        sibling_copy(zz).wait_recv()
        add_rows(part, zz * plane_rows, plane_rows, [(sib_in, None, zz * plane_rows)])
        for aa in range(2):
            last_copy(zz, aa).start()

    def reduce_z(zz, final):
        for aa in range(2):
            start = index(aa, b, zz) * rows
            last_copy(zz, aa).wait_recv()
            add_rows(part, start, rows, [(from_last, zz * 2 + aa, 0)])
            for way in range(2):
                reached = (z > 0) if way == 0 else (z < 3)
                ours = True if final else (zz > z if way == 0 else zz < z)

                @pl.when(jnp.logical_and(reached, ours))
                def _():
                    z_copy(way, zz, aa).wait_recv()
                    add_rows(part, start, rows, [(from_z, way * 8 + zz * 2 + aa, 0)])

                if not final:
                    pl.when(ours)(z_copy(way, zz, aa).start)

    def first_copy():
        return pltpu.make_async_remote_copy(
            src_ref=part.at[block(first)], dst_ref=from_first, send_sem=first_send, recv_sem=first_recv,
            **where(first, c))

    outs = (gg_ref, gu_ref, gd_ref)

    def weight_grad(m, h):
        lhs = act_t if m < 2 else hid_t
        base = m * hidden if m < 2 else 0
        rhs = xs if m < 2 else ds_

        @pl.loop(0, half // 512)
        def _(j):
            cols = pl.ds(pl.multiple_of(j * 512, 512), 512)
            stage[m, h, :, cols] = jnp.dot(
                lhs[pl.ds(base, hidden), :], rhs[h, :, cols], preferred_element_type=f32).astype(jnp.bfloat16)

        weight_copy(m, h).start()

    def weight_copy(m, h):
        return pltpu.make_async_copy(
            stage.at[m, h], outs[m].at[0, :, pl.ds(h * half, half)], out_sem.at[m, h])

    planes = [plane_of(q) for q in range(4)]
    backward(planes[0])
    backward(planes[1])
    reduce_last(planes[0])
    backward(planes[2])
    reduce_last(planes[1])
    reduce_z(planes[0], False)
    backward(planes[3])
    reduce_last(planes[2])
    reduce_z(planes[1], False)
    reduce_last(planes[3])
    act_t[...] = act[...].T
    weight_grad(0, 0)
    weight_grad(0, 1)
    reduce_z(planes[2], False)
    weight_grad(1, 0)
    weight_grad(1, 1)
    hid_t[...] = hid[...].T
    weight_grad(2, 0)
    weight_grad(2, 1)
    reduce_z(planes[3], True)
    first_copy().start()
    first_copy().wait_recv()

    @pl.loop(0, rows // 16)
    def _(i):
        here = pl.ds(pl.multiple_of(i * 16, 16), 16)
        mine = pl.ds(pl.multiple_of(e * rows + i * 16, 16), 16)
        out_ref[here, :] = (part[mine, :].astype(f32) + from_first[here, :].astype(f32)).astype(jnp.bfloat16)

    for m in range(3):
        for h in range(2):
            weight_copy(m, h).wait()
    first_copy().wait_send()
    for q in range(4):
        sibling_copy(planes[q]).wait_send()
        for aa in range(2):
            last_copy(planes[q], aa).wait_send()
            if q < 3:
                pl.when(planes[q] > z)(z_copy(0, planes[q], aa).wait_send)
                pl.when(planes[q] < z)(z_copy(1, planes[q], aa).wait_send)
    gather_sent(0)
    gather_sent(1)


def on_device_tree(tokens, cotangent, expert_ids, gate_values, w_gate, w_up, w_down):
    rows, half = tokens.shape
    hidden = w_gate.shape[1]
    experts = lax.axis_size("expert")
    total = rows * experts
    chosen = expert_ids[:, :, None] == jnp.arange(experts, dtype=jnp.int32)[None, None, :]
    dense = jnp.sum(jnp.where(chosen, gate_values[:, :, None], 0.0), axis=1)
    high = lax.reduce_precision(dense, 8, 7)
    middle = lax.reduce_precision(dense - high, 8, 7)
    low = dense - high - middle
    gates = jnp.concatenate(
        [high, middle, low, jnp.zeros((rows, 128 - 3 * experts), jnp.float32)], axis=1).astype(jnp.bfloat16)
    bf16, f32 = jnp.bfloat16, jnp.float32
    any_, vmem = pl.BlockSpec(memory_space=pl.ANY), pl.BlockSpec(memory_space=pltpu.VMEM)
    dma = pltpu.SemaphoreType.DMA
    return tuple(pl.pallas_call(
        merge_kernel,
        out_shape=(
            jax.ShapeDtypeStruct(tokens.shape, bf16),
            jax.ShapeDtypeStruct(w_gate.shape, bf16),
            jax.ShapeDtypeStruct(w_up.shape, bf16),
            jax.ShapeDtypeStruct(w_down.shape, bf16),
        ),
        in_specs=[any_, any_, vmem, any_, any_, any_],
        out_specs=(vmem, any_, any_, any_),
        scratch_shapes=[
            pltpu.VMEM((2, total, half), bf16),
            pltpu.VMEM((2, total, half + 128), bf16),
            pltpu.VMEM((2, 2 * hidden, half), bf16),
            pltpu.VMEM((2, hidden, half), bf16),
            pltpu.VMEM((total, 2 * hidden), f32),
            pltpu.VMEM((4 * rows, hidden), f32),
            pltpu.VMEM((total, 2 * hidden), bf16),
            pltpu.VMEM((total, hidden), bf16),
            pltpu.VMEM((2 * hidden, total), bf16),
            pltpu.VMEM((hidden, total), bf16),
            pltpu.VMEM((total, half), bf16),
            pltpu.VMEM((total, half), bf16),
            pltpu.VMEM((total, half), bf16),
            pltpu.VMEM((8, rows, half), bf16),
            pltpu.VMEM((16, rows, half), bf16),
            pltpu.VMEM((rows, half), bf16),
            pltpu.VMEM((3, 2, hidden, half), bf16),
            dma((8,)),
            dma((2, 5, 16)),
            dma((2, 2, 16)),
            dma((4,)),
            dma((4,)),
            dma((8,)),
            dma((8,)),
            dma((16,)),
            dma((16,)),
            dma,
            dma,
            dma((3, 2)),
        ],
        compiler_params=pltpu.CompilerParams(
            collective_id=0, has_side_effects=True, vmem_limit_bytes=62 * 1024 * 1024),
        cost_estimate=pl.CostEstimate(
            flops=16 * total * hidden * 2 * half, bytes_accessed=24 * hidden * half, transcendentals=total * hidden),
    )(tokens, cotangent, gates, w_gate, w_up, w_down))


def solution(mesh):
    tree = mesh.shape["expert"] == 16 and mesh.shape["tensor"] == 2
    return jax.shard_map(
        on_device_tree if tree else on_device,
        mesh=mesh,
        in_specs=(
            P("expert", "tensor"),
            P("expert", "tensor"),
            P("expert", None),
            P("expert", None),
            P("expert", "tensor", None),
            P("expert", "tensor", None),
            P("expert", "tensor", None),
        ),
        out_specs=(
            P("expert", "tensor"),
            P("expert", "tensor", None),
            P("expert", "tensor", None),
            P("expert", "tensor", None),
        ),
        check_vma=False,
    )
```

```python
import functools

import jax
import jax.numpy as jnp
from jax import lax
from jax.experimental import pallas as pl
from jax.experimental.pallas import tpu as pltpu
from jax.sharding import PartitionSpec as P

TOP = 8
MESH = pl.DeviceIdType.MESH


def expert_backward(rows_x, rows_d, w_gate, w_up, w_down):
    gate_pre = jnp.einsum("secd,ehd->sech", rows_x, w_gate, preferred_element_type=jnp.float32)
    up_pre = jnp.einsum("secd,ehd->sech", rows_x, w_up, preferred_element_type=jnp.float32)
    sigmoid = jax.nn.sigmoid(gate_pre)
    active = gate_pre * sigmoid
    hidden = (active * up_pre).astype(jnp.bfloat16)
    hidden_grad = jnp.einsum("secd,ehd->sech", rows_d, w_down, preferred_element_type=jnp.float32)
    up_grad = (hidden_grad * active).astype(jnp.bfloat16)
    gate_grad = (hidden_grad * up_pre * sigmoid * (1.0 + gate_pre * (1.0 - sigmoid))).astype(
        jnp.bfloat16
    )
    grad_gate = jnp.einsum(
        "sech,secd->ehd", gate_grad, rows_x, preferred_element_type=jnp.float32
    ).astype(jnp.bfloat16)
    grad_up = jnp.einsum(
        "sech,secd->ehd", up_grad, rows_x, preferred_element_type=jnp.float32
    ).astype(jnp.bfloat16)
    grad_down = jnp.einsum(
        "sech,secd->ehd", hidden, rows_d, preferred_element_type=jnp.float32
    ).astype(jnp.bfloat16)
    partial_value = jnp.einsum(
        "sech,ehd->secd", gate_grad, w_gate, preferred_element_type=jnp.float32
    )
    partial_value = partial_value + jnp.einsum(
        "sech,ehd->secd", up_grad, w_up, preferred_element_type=jnp.float32
    )
    return (partial_value, grad_gate, grad_up, grad_down)


def on_device(tokens, cotangent, expert_ids, gate_values, w_gate, w_up, w_down):
    tok_count = expert_ids.shape[0]
    local_count = w_gate.shape[0]
    groups = lax.axis_size("expert")
    experts = local_count * groups
    capacity = 4 * tok_count * TOP // (3 * experts)
    feat_width = tokens.shape[1]
    flat_ids = expert_ids.reshape(-1)
    onehot = (flat_ids[:, None] == jnp.arange(experts, dtype=jnp.int32)[None, :]).astype(jnp.int32)
    before = jnp.cumsum(onehot, axis=0) - onehot
    slot_pos = jnp.sum(before * onehot, axis=1)
    target = flat_ids * capacity + slot_pos
    matches = (target[None, :] == jnp.arange(experts * capacity, dtype=jnp.int32)[:, None]).reshape(
        experts * capacity, tok_count, TOP
    )
    by_token = jnp.any(matches, axis=2)
    occupied = jnp.any(by_token, axis=1)
    token_iota = jnp.arange(tok_count, dtype=jnp.int32)
    owner = jnp.sum(jnp.where(by_token, token_iota[None, :], 0), axis=1)
    slot_weight = jnp.sum(jnp.sum(jnp.where(matches, gate_values[None, :, :], 0.0), axis=2), axis=1)
    full_x, full_d = (
        lax.all_gather(tokens, "tensor", axis=1, tiled=True),
        lax.all_gather(cotangent, "tensor", axis=1, tiled=True),
    )
    sent_x = jnp.where(occupied[:, None], full_x[owner], jnp.zeros((), jnp.bfloat16))
    sent_d = (slot_weight[:, None] * full_d[owner].astype(jnp.float32)).astype(jnp.bfloat16)
    buffer_shape = (groups, local_count, capacity, full_x.shape[1])
    sent_x, sent_d = (sent_x.reshape(buffer_shape), sent_d.reshape(buffer_shape))
    rows_x, rows_d = (
        lax.all_to_all(sent_x, "expert", split_axis=0, concat_axis=0, tiled=True),
        lax.all_to_all(sent_d, "expert", split_axis=0, concat_axis=0, tiled=True),
    )
    partial_value, grad_gate, grad_up, grad_down = expert_backward(
        rows_x, rows_d, w_gate, w_up, w_down
    )
    summed = lax.psum(partial_value.astype(jnp.bfloat16), "tensor").astype(jnp.float32)
    returned = lax.dynamic_slice_in_dim(
        summed, lax.axis_index("tensor") * feat_width, feat_width, 3
    ).astype(jnp.bfloat16)
    arrived = lax.all_to_all(returned, "expert", split_axis=0, concat_axis=0, tiled=True).reshape(
        experts * capacity, feat_width
    )
    masked = jnp.where(occupied[:, None], arrived.astype(jnp.float32), jnp.zeros((), jnp.float32))
    grad_tokens = jax.ops.segment_sum(masked, owner, num_segments=tok_count).astype(jnp.bfloat16)
    return (grad_tokens, grad_gate, grad_up, grad_down)


def merge_kernel(
    sizes, tok_ref, cot_ref, gate_ref, wg_ref, wu_ref, wd_ref,
    out_ref, gg_ref, gu_ref, gd_ref,
    xs, ds_, wgu, wd, pre, hgrad, act, hid, act_t, hid_t, part, sib_out, sib_in, from_last, from_z, from_first,
    load_sem, send, recv, sib_send, sib_recv, last_send, last_recv, z_send, z_recv, first_send, first_recv, out_sem,
):
    half = tok_ref.shape[1]
    hidden = wg_ref.shape[1]
    f32 = jnp.float32
    starts = (0, sizes[0])
    e, c = lax.axis_index("expert"), lax.axis_index("tensor")
    x, y, z = e % 2, (e // 2) % 2, e // 4
    a, b = x + c * (y - x), y + c * (x - y)

    def index(aa, bb, zz):
        return zz * 4 + aa * (1 + c) + bb * (2 - c)

    def where(expert, core):
        return dict(device_id={"expert": expert, "tensor": core}, device_id_type=MESH)

    first, last = index(1 - a, b, z), index(a, 1 - b, z)
    up, down = e + 4, e - 4
    bufs = (xs, ds_)

    def block(j, blk):
        return pl.ds(pl.multiple_of(blk * sizes[j], 16), sizes[j])

    loads = []
    for t, ref in enumerate((tok_ref, cot_ref)):
        for j in range(2):
            loads.append(pltpu.make_async_copy(
                ref.at[pl.ds(starts[j], sizes[j])],
                bufs[t][j].at[c, block(j, e), pl.ds(0, half)], load_sem.at[t * 2 + j]))
    n = 4
    weights = []
    for h in range(2):
        cols = pl.ds(h * half, half)
        weights.append(pltpu.make_async_copy(wg_ref.at[0, :, cols], wgu.at[h, pl.ds(0, hidden)], load_sem.at[n]))
        weights.append(pltpu.make_async_copy(wu_ref.at[0, :, cols], wgu.at[h, pl.ds(hidden, hidden)], load_sem.at[n + 1]))
        weights.append(pltpu.make_async_copy(wd_ref.at[0, :, cols], wd.at[h], load_sem.at[n + 2]))
        n += 3
    for copy in loads + weights:
        copy.start()
    for j in range(2):
        ds_[j][c, block(j, e), half:] = gate_ref[starts[j]:starts[j] + sizes[j], :]

    barrier = pltpu.get_barrier_semaphore()
    pl.semaphore_signal(barrier, inc=1, **where(first, c))
    pl.semaphore_signal(barrier, inc=1, **where(last, c))
    pl.semaphore_signal(barrier, inc=1, **where(e, 1 - c))

    @pl.when(z < 3)
    def _():
        pl.semaphore_signal(barrier, inc=1, **where(up, c))

    @pl.when(z > 0)
    def _():
        pl.semaphore_signal(barrier, inc=1, **where(down, c))

    pl.semaphore_wait(barrier, 4 + (z + 1) // 2 % 2)
    for copy in loads:
        copy.wait()

    def gather_copy(t, j, kind, blk, core):
        target = (first, up, down, last, e)[kind]
        view = bufs[t][j].at[core, block(j, blk)]
        return pltpu.make_async_remote_copy(
            src_ref=view, dst_ref=view, send_sem=send.at[t * 2 + j, kind, blk],
            recv_sem=recv.at[t * 2 + j, kind // 4, blk], **where(target, 1 - c if kind == 4 else c))

    def arrive(t, j, blk):
        gather_copy(t, j, 0, blk, c).wait_recv()

    def each(t, j, blk, kinds, verb):
        for kind in kinds:
            do = getattr(gather_copy(t, j, kind, blk, c), verb)
            if kind == 1:
                pl.when(z < 3)(do)
            elif kind == 2:
                pl.when(z > 0)(do)
            else:
                do()

    def own(t, j):
        each(t, j, e, (0, 1, 2, 3, 4), "start")

    def first_step(t, j):
        blk = index(1 - a, b, z)
        arrive(t, j, blk)
        each(t, j, blk, (1, 2, 3, 4), "start")

    def z_step(t, j, k):
        for aa in (a, 1 - a):
            @pl.when(z >= k)
            def _():
                blk = index(aa, b, z - k)
                arrive(t, j, blk)
                each(t, j, blk, (1, 3, 4), "start")

            @pl.when(z + k <= 3)
            def _():
                blk = index(aa, b, z + k)
                arrive(t, j, blk)
                each(t, j, blk, (2, 3, 4), "start")

    def last_step(t, j, k):
        def over(blk):
            arrive(t, j, blk)
            each(t, j, blk, (4,), "start")

        for aa in (a, 1 - a):
            if k == 0:
                over(index(aa, 1 - b, z))
                continue

            @pl.when(z >= k)
            def _():
                over(index(aa, 1 - b, z - k))

            @pl.when(z + k <= 3)
            def _():
                over(index(aa, 1 - b, z + k))

    def sibling_step(t, j):
        @pl.loop(0, 16)
        def _(blk):
            gather_copy(t, j, 4, blk, 1 - c).wait_recv()

    def gather_sent(t, j):
        each(t, j, e, (0, 1, 2, 3, 4), "wait_send")
        each(t, j, index(1 - a, b, z), (1, 2, 3, 4), "wait_send")
        for k in range(1, 4):
            for aa in (a, 1 - a):
                pl.when(z >= k)(lambda: each(t, j, index(aa, b, z - k), (1, 3, 4), "wait_send"))
                pl.when(z + k <= 3)(lambda: each(t, j, index(aa, b, z + k), (2, 3, 4), "wait_send"))

        @pl.loop(0, 4)
        def _(zz):
            for aa in range(2):
                gather_copy(t, j, 4, index(aa, 1 - b, zz), c).wait_send()

    contract_last = (((1,), (1,)), ((), ()))

    def rows_of(j):
        return pl.ds(starts[j] * 16, sizes[j] * 16)

    def forward(j, lo, hi):
        @pl.loop(lo, hi)
        def _(i):
            cols = pl.ds(pl.multiple_of(i * 256, 256), 256)
            pre[rows_of(j), cols] = lax.dot_general(
                xs[j][0], wgu[0, cols, :], contract_last, preferred_element_type=f32
            ) + lax.dot_general(xs[j][1], wgu[1, cols, :], contract_last, preferred_element_type=f32)

    def hidden_backward(j):
        @pl.loop(0, sizes[j] * 16 // 256)
        def _(i):
            at = pl.ds(pl.multiple_of(i * 256, 256), 256)
            hgrad[at, :] = lax.dot_general(
                ds_[j][0, at, pl.ds(0, half)], wd[0], contract_last, preferred_element_type=f32
            ) + lax.dot_general(ds_[j][1, at, pl.ds(0, half)], wd[1], contract_last, preferred_element_type=f32)

        @pl.loop(0, sizes[j] * 16 // 64)
        def _(i):
            there = pl.ds(pl.multiple_of(i * 64, 64), 64)
            here = pl.ds(pl.multiple_of(starts[j] * 16 + i * 64, 64), 64)
            lane = lax.broadcasted_iota(jnp.int32, (64, 128), 1)
            pieces = ds_[j][0, there, pl.ds(half, 128)].astype(f32)
            weight = jnp.sum(jnp.where(jnp.bitwise_and(lane, 15) == e, pieces, 0.0), axis=1, keepdims=True)
            gate_pre, up_pre = pre[here, pl.ds(0, hidden)], pre[here, pl.ds(hidden, hidden)]
            sigmoid = 1.0 / (1.0 + jnp.exp(-gate_pre))
            active = gate_pre * sigmoid
            grad = hgrad[there, :] * weight
            hid[here, :] = (active * up_pre * weight).astype(jnp.bfloat16)
            act[here, pl.ds(hidden, hidden)] = (grad * active).astype(jnp.bfloat16)
            act[here, pl.ds(0, hidden)] = (
                grad * up_pre * sigmoid * (1.0 + gate_pre * (1.0 - sigmoid))).astype(jnp.bfloat16)

    def row_backward(j, side, dest):
        @pl.loop(0, half // 512)
        def _(i):
            cols = pl.ds(pl.multiple_of(i * 512, 512), 512)
            dest[j][:, cols] = jnp.dot(
                act[rows_of(j), :], wgu[side, :, cols], preferred_element_type=f32).astype(jnp.bfloat16)

    def plane_of(q):
        swapped = (0, 1, 3, 2)[q]
        turn = q + ((z + 1) // 2 % 2) * (swapped - q)
        high = z // 2
        return high * turn + (1 - high) * (3 - turn)

    planes = [plane_of(q) for q in range(4)]

    def sibling_copy(j, zz):
        at = pl.ds(pl.multiple_of(zz * 4 * sizes[j], 16), 4 * sizes[j])
        return pltpu.make_async_remote_copy(
            src_ref=sib_out[j].at[at], dst_ref=sib_in[j].at[at], send_sem=sib_send.at[j, zz],
            recv_sem=sib_recv.at[j, zz], **where(e, 1 - c))

    def row_backward_out(j):
        row_backward(j, 1 - c, sib_out)
        for zz in planes:
            sibling_copy(j, zz).start()

    def row_backward_own(j):
        row_backward(j, c, part)

    def add_rows(j, start, count, sources):
        dest = part[j]

        @pl.loop(0, count // 16)
        def _(i):
            here = pl.ds(pl.multiple_of(start + i * 16, 16), 16)
            total = dest[here, :].astype(f32)
            for ref, lead, offset in sources:
                there = pl.ds(pl.multiple_of(offset + i * 16, 16), 16)
                total = total + (ref[there, :] if lead is None else ref[lead, there, :]).astype(f32)
            dest[here, :] = total.astype(jnp.bfloat16)

    def last_copy(j, zz, aa):
        slot = zz * 2 + aa
        return pltpu.make_async_remote_copy(
            src_ref=part[j].at[block(j, index(aa, 1 - b, zz))], dst_ref=from_last[j].at[slot],
            send_sem=last_send.at[j, slot], recv_sem=last_recv.at[j, slot], **where(last, c))

    def z_copy(j, way, zz, aa):
        slot = way * 8 + zz * 2 + aa
        return pltpu.make_async_remote_copy(
            src_ref=part[j].at[block(j, index(aa, b, zz))], dst_ref=from_z[j].at[slot],
            send_sem=z_send.at[j, slot], recv_sem=z_recv.at[j, slot], **where(down if way else up, c))

    def reduce_last(j, q):
        zz = planes[q]
        sibling_copy(j, zz).wait_recv()
        add_rows(j, zz * 4 * sizes[j], 4 * sizes[j], [(sib_in[j], None, zz * 4 * sizes[j])])
        for aa in range(2):
            last_copy(j, zz, aa).start()

    def reduce_z(j, q):
        zz, final = planes[q], q == 3
        for aa in range(2):
            start = index(aa, b, zz) * sizes[j]
            last_copy(j, zz, aa).wait_recv()
            add_rows(j, start, sizes[j], [(from_last[j], zz * 2 + aa, 0)])
            for way in range(2):
                reached = (z > 0) if way == 0 else (z < 3)
                ours = True if final else (zz > z if way == 0 else zz < z)

                @pl.when(jnp.logical_and(reached, ours))
                def _():
                    z_copy(j, way, zz, aa).wait_recv()
                    add_rows(j, start, sizes[j], [(from_z[j], way * 8 + zz * 2 + aa, 0)])

                if not final:
                    pl.when(ours)(z_copy(j, way, zz, aa).start)

    def first_copy(j):
        return pltpu.make_async_remote_copy(
            src_ref=part[j].at[block(j, first)], dst_ref=from_first[j], send_sem=first_send.at[j],
            recv_sem=first_recv.at[j], **where(first, c))

    def finish(j):
        first_copy(j).wait_recv()

        @pl.loop(0, sizes[j] // 16)
        def _(i):
            here = pl.ds(pl.multiple_of(i * 16, 16), 16)
            mine = pl.ds(pl.multiple_of(e * sizes[j] + i * 16, 16), 16)
            out_ref[pl.ds(pl.multiple_of(starts[j] + i * 16, 16), 16), :] = (
                part[j][mine, :].astype(f32) + from_first[j][here, :].astype(f32)).astype(jnp.bfloat16)

    outs = (gg_ref, gu_ref, gd_ref)

    def weight_copy(m, h):
        held = wgu.at[h, pl.ds(m * hidden, hidden)] if m < 2 else wd.at[h]
        return pltpu.make_async_copy(held, outs[m].at[0, :, pl.ds(h * half, half)], out_sem.at[m, h])

    def weight_grad(m, h):
        lhs, rhs = (act_t, xs) if m < 2 else (hid_t, ds_)
        base = m * hidden if m < 2 else 0

        @pl.loop(0, half // 512)
        def _(i):
            cols = pl.ds(pl.multiple_of(i * 512, 512), 512)
            total = jnp.dot(
                lhs[pl.ds(base, hidden), rows_of(0)], rhs[0][h, :, cols], preferred_element_type=f32
            ) + jnp.dot(lhs[pl.ds(base, hidden), rows_of(1)], rhs[1][h, :, cols], preferred_element_type=f32)
            if m < 2:
                wgu[h, pl.ds(base, hidden), cols] = total.astype(jnp.bfloat16)
            else:
                wd[h, :, cols] = total.astype(jnp.bfloat16)

        weight_copy(m, h).start()

    X, G = 0, 1
    own(X, 0)
    first_step(X, 0)
    z_step(X, 0, 1)
    own(G, 0)
    last_step(X, 0, 0)
    z_step(X, 0, 2)
    last_step(X, 0, 1)
    z_step(X, 0, 3)
    first_step(G, 0)
    last_step(X, 0, 2)
    z_step(G, 0, 1)
    last_step(X, 0, 3)
    last_step(G, 0, 0)
    own(X, 1)
    for copy in weights:
        copy.wait()
    sibling_step(X, 0)
    z_step(G, 0, 2)
    forward(0, 0, 1)
    last_step(G, 0, 1)
    z_step(G, 0, 3)
    first_step(X, 1)
    own(G, 1)
    forward(0, 1, 2)
    last_step(G, 0, 2)
    z_step(X, 1, 1)
    forward(0, 2, 3)
    last_step(G, 0, 3)
    last_step(X, 1, 0)
    sibling_step(G, 0)

    hidden_backward(0)
    z_step(X, 1, 2)
    last_step(X, 1, 1)
    first_step(G, 1)
    row_backward_out(0)
    z_step(X, 1, 3)
    last_step(X, 1, 2)
    z_step(G, 1, 1)
    row_backward_own(0)
    last_step(X, 1, 3)
    last_step(G, 1, 0)
    reduce_last(0, 0)
    z_step(G, 1, 2)
    reduce_last(0, 1)
    last_step(G, 1, 1)
    reduce_z(0, 0)
    sibling_step(X, 1)
    z_step(G, 1, 3)
    reduce_last(0, 2)
    reduce_z(0, 1)
    last_step(G, 1, 2)
    reduce_last(0, 3)
    forward(1, 0, 3)
    last_step(G, 1, 3)
    reduce_z(0, 2)
    sibling_step(G, 1)

    hidden_backward(1)
    row_backward_out(1)
    row_backward_own(1)
    reduce_last(1, 0)
    reduce_last(1, 1)
    reduce_z(0, 3)
    first_copy(0).start()
    reduce_last(1, 2)
    reduce_z(1, 0)
    reduce_last(1, 3)
    act_t[...] = act[...].T
    weight_grad(0, 0)
    reduce_z(1, 1)
    weight_grad(0, 1)
    weight_grad(1, 0)
    reduce_z(1, 2)
    weight_grad(1, 1)
    finish(0)
    hid_t[...] = hid[...].T
    reduce_z(1, 3)
    first_copy(1).start()
    weight_grad(2, 0)
    weight_grad(2, 1)
    finish(1)

    for m in range(3):
        for h in range(2):
            weight_copy(m, h).wait()
    for j in range(2):
        first_copy(j).wait_send()
        for q in range(4):
            zz = planes[q]
            sibling_copy(j, zz).wait_send()
            for aa in range(2):
                last_copy(j, zz, aa).wait_send()
                if q < 3:
                    pl.when(zz > z)(z_copy(j, 0, zz, aa).wait_send)
                    pl.when(zz < z)(z_copy(j, 1, zz, aa).wait_send)
        gather_sent(0, j)
        gather_sent(1, j)


def on_device_tree(tokens, cotangent, expert_ids, gate_values, w_gate, w_up, w_down):
    rows, half = tokens.shape
    hidden = w_gate.shape[1]
    experts = lax.axis_size("expert")
    total = rows * experts
    sizes = (rows // 48 * 32, rows // 48 * 16)
    chosen = expert_ids[:, :, None] == jnp.arange(experts, dtype=jnp.int32)[None, None, :]
    dense = jnp.sum(jnp.where(chosen, gate_values[:, :, None], 0.0), axis=1)
    high = lax.reduce_precision(dense, 8, 7)
    middle = lax.reduce_precision(dense - high, 8, 7)
    low = dense - high - middle
    gates = jnp.concatenate(
        [high, middle, low, jnp.zeros((rows, 128 - 3 * experts), jnp.float32)], axis=1).astype(jnp.bfloat16)
    bf16, f32 = jnp.bfloat16, jnp.float32
    any_, vmem = pl.BlockSpec(memory_space=pl.ANY), pl.BlockSpec(memory_space=pltpu.VMEM)
    dma = pltpu.SemaphoreType.DMA
    whole = tuple(size * experts for size in sizes)

    def chunks(*shape):
        return [pltpu.VMEM(tuple(n[j] if isinstance(n, tuple) else n for n in shape), bf16) for j in range(2)]

    return tuple(pl.pallas_call(
        functools.partial(merge_kernel, sizes),
        out_shape=(
            jax.ShapeDtypeStruct(tokens.shape, bf16),
            jax.ShapeDtypeStruct(w_gate.shape, bf16),
            jax.ShapeDtypeStruct(w_up.shape, bf16),
            jax.ShapeDtypeStruct(w_down.shape, bf16),
        ),
        in_specs=[any_, any_, vmem, any_, any_, any_],
        out_specs=(vmem, any_, any_, any_),
        scratch_shapes=[
            chunks(2, whole, half),
            chunks(2, whole, half + 128),
            pltpu.VMEM((2, 2 * hidden, half), bf16),
            pltpu.VMEM((2, hidden, half), bf16),
            pltpu.VMEM((total, 2 * hidden), f32),
            pltpu.VMEM((whole[0], hidden), f32),
            pltpu.VMEM((total, 2 * hidden), bf16),
            pltpu.VMEM((total, hidden), bf16),
            pltpu.VMEM((2 * hidden, total), bf16),
            pltpu.VMEM((hidden, total), bf16),
            chunks(whole, half),
            chunks(whole, half),
            chunks(whole, half),
            chunks(8, sizes, half),
            chunks(16, sizes, half),
            chunks(sizes, half),
            dma((10,)),
            dma((4, 5, 16)),
            dma((4, 2, 16)),
            dma((2, 4)),
            dma((2, 4)),
            dma((2, 8)),
            dma((2, 8)),
            dma((2, 16)),
            dma((2, 16)),
            dma((2,)),
            dma((2,)),
            dma((3, 2)),
        ],
        compiler_params=pltpu.CompilerParams(
            collective_id=0, has_side_effects=True, vmem_limit_bytes=43 * 1024 * 1024),
        cost_estimate=pl.CostEstimate(
            flops=16 * total * hidden * 2 * half, bytes_accessed=24 * hidden * half, transcendentals=total * hidden),
    )(tokens, cotangent, gates, w_gate, w_up, w_down))


def solution(mesh):
    tree = mesh.shape["expert"] == 16 and mesh.shape["tensor"] == 2
    return jax.shard_map(
        on_device_tree if tree else on_device,
        mesh=mesh,
        in_specs=(
            P("expert", "tensor"),
            P("expert", "tensor"),
            P("expert", None),
            P("expert", None),
            P("expert", "tensor", None),
            P("expert", "tensor", None),
            P("expert", "tensor", None),
        ),
        out_specs=(
            P("expert", "tensor"),
            P("expert", "tensor", None),
            P("expert", "tensor", None),
            P("expert", "tensor", None),
        ),
        check_vma=False,
    )
```

```python
import functools

import jax
import jax.numpy as jnp
from jax import lax
from jax.experimental import pallas as pl
from jax.experimental.pallas import tpu as pltpu
from jax.sharding import PartitionSpec as P

TOP = 8
MESH = pl.DeviceIdType.MESH


def expert_backward(rows_x, rows_d, w_gate, w_up, w_down):
    gate_pre = jnp.einsum("secd,ehd->sech", rows_x, w_gate, preferred_element_type=jnp.float32)
    up_pre = jnp.einsum("secd,ehd->sech", rows_x, w_up, preferred_element_type=jnp.float32)
    sigmoid = jax.nn.sigmoid(gate_pre)
    active = gate_pre * sigmoid
    hidden = (active * up_pre).astype(jnp.bfloat16)
    hidden_grad = jnp.einsum("secd,ehd->sech", rows_d, w_down, preferred_element_type=jnp.float32)
    up_grad = (hidden_grad * active).astype(jnp.bfloat16)
    gate_grad = (hidden_grad * up_pre * sigmoid * (1.0 + gate_pre * (1.0 - sigmoid))).astype(
        jnp.bfloat16
    )
    grad_gate = jnp.einsum(
        "sech,secd->ehd", gate_grad, rows_x, preferred_element_type=jnp.float32
    ).astype(jnp.bfloat16)
    grad_up = jnp.einsum(
        "sech,secd->ehd", up_grad, rows_x, preferred_element_type=jnp.float32
    ).astype(jnp.bfloat16)
    grad_down = jnp.einsum(
        "sech,secd->ehd", hidden, rows_d, preferred_element_type=jnp.float32
    ).astype(jnp.bfloat16)
    partial_value = jnp.einsum(
        "sech,ehd->secd", gate_grad, w_gate, preferred_element_type=jnp.float32
    )
    partial_value = partial_value + jnp.einsum(
        "sech,ehd->secd", up_grad, w_up, preferred_element_type=jnp.float32
    )
    return (partial_value, grad_gate, grad_up, grad_down)


def on_device(tokens, cotangent, expert_ids, gate_values, w_gate, w_up, w_down):
    tok_count = expert_ids.shape[0]
    local_count = w_gate.shape[0]
    groups = lax.axis_size("expert")
    experts = local_count * groups
    capacity = 4 * tok_count * TOP // (3 * experts)
    feat_width = tokens.shape[1]
    flat_ids = expert_ids.reshape(-1)
    onehot = (flat_ids[:, None] == jnp.arange(experts, dtype=jnp.int32)[None, :]).astype(jnp.int32)
    before = jnp.cumsum(onehot, axis=0) - onehot
    slot_pos = jnp.sum(before * onehot, axis=1)
    target = flat_ids * capacity + slot_pos
    matches = (target[None, :] == jnp.arange(experts * capacity, dtype=jnp.int32)[:, None]).reshape(
        experts * capacity, tok_count, TOP
    )
    by_token = jnp.any(matches, axis=2)
    occupied = jnp.any(by_token, axis=1)
    token_iota = jnp.arange(tok_count, dtype=jnp.int32)
    owner = jnp.sum(jnp.where(by_token, token_iota[None, :], 0), axis=1)
    slot_weight = jnp.sum(jnp.sum(jnp.where(matches, gate_values[None, :, :], 0.0), axis=2), axis=1)
    full_x, full_d = (
        lax.all_gather(tokens, "tensor", axis=1, tiled=True),
        lax.all_gather(cotangent, "tensor", axis=1, tiled=True),
    )
    sent_x = jnp.where(occupied[:, None], full_x[owner], jnp.zeros((), jnp.bfloat16))
    sent_d = (slot_weight[:, None] * full_d[owner].astype(jnp.float32)).astype(jnp.bfloat16)
    buffer_shape = (groups, local_count, capacity, full_x.shape[1])
    sent_x, sent_d = (sent_x.reshape(buffer_shape), sent_d.reshape(buffer_shape))
    rows_x, rows_d = (
        lax.all_to_all(sent_x, "expert", split_axis=0, concat_axis=0, tiled=True),
        lax.all_to_all(sent_d, "expert", split_axis=0, concat_axis=0, tiled=True),
    )
    partial_value, grad_gate, grad_up, grad_down = expert_backward(
        rows_x, rows_d, w_gate, w_up, w_down
    )
    summed = lax.psum(partial_value.astype(jnp.bfloat16), "tensor").astype(jnp.float32)
    returned = lax.dynamic_slice_in_dim(
        summed, lax.axis_index("tensor") * feat_width, feat_width, 3
    ).astype(jnp.bfloat16)
    arrived = lax.all_to_all(returned, "expert", split_axis=0, concat_axis=0, tiled=True).reshape(
        experts * capacity, feat_width
    )
    masked = jnp.where(occupied[:, None], arrived.astype(jnp.float32), jnp.zeros((), jnp.float32))
    grad_tokens = jax.ops.segment_sum(masked, owner, num_segments=tok_count).astype(jnp.bfloat16)
    return (grad_tokens, grad_gate, grad_up, grad_down)


def merge_kernel(
    sizes, tok_ref, cot_ref, gate_ref, wg_ref, wu_ref, wd_ref,
    out_ref, gg_ref, gu_ref, gd_ref,
    xs, ds_, wgu, wd, pre, hgrad, act, hid, act_t, hid_t, part, sib_out, sib_in, from_last, from_z, from_first,
    acc, load_sem, send, recv, sib_send, sib_recv, last_send, last_recv, z_send, z_recv, first_send, first_recv, out_sem,
):
    half = tok_ref.shape[1]
    hidden = wg_ref.shape[1]
    f32 = jnp.float32
    count = len(sizes)
    starts = tuple(sum(sizes[:j]) for j in range(count))
    e, c = lax.axis_index("expert"), lax.axis_index("tensor")
    x, y, z = e % 2, (e // 2) % 2, e // 4
    a, b = x + c * (y - x), y + c * (x - y)

    def index(aa, bb, zz):
        return zz * 4 + aa * (1 + c) + bb * (2 - c)

    def where(expert, core):
        return dict(device_id={"expert": expert, "tensor": core}, device_id_type=MESH)

    first, last = index(1 - a, b, z), index(a, 1 - b, z)
    up, down = e + 4, e - 4
    bufs = (xs, ds_)

    def block(j, blk):
        return pl.ds(pl.multiple_of(blk * sizes[j], 16), sizes[j])

    loads = []
    for t, ref in enumerate((tok_ref, cot_ref)):
        for j in range(count):
            loads.append(pltpu.make_async_copy(
                ref.at[pl.ds(starts[j], sizes[j])],
                bufs[t][j].at[c, block(j, e), pl.ds(0, half)], load_sem.at[t * count + j]))
    n = 2 * count
    weights = []
    for h in range(2):
        cols = pl.ds(h * half, half)
        weights.append(pltpu.make_async_copy(wg_ref.at[0, :, cols], wgu.at[h, pl.ds(0, hidden)], load_sem.at[n]))
        weights.append(pltpu.make_async_copy(wu_ref.at[0, :, cols], wgu.at[h, pl.ds(hidden, hidden)], load_sem.at[n + 1]))
        weights.append(pltpu.make_async_copy(wd_ref.at[0, :, cols], wd.at[h], load_sem.at[n + 2]))
        n += 3
    for copy in loads + weights:
        copy.start()
    for j in range(count):
        ds_[j][c, block(j, e), half:] = gate_ref[starts[j]:starts[j] + sizes[j], :]

    barrier = pltpu.get_barrier_semaphore()
    pl.semaphore_signal(barrier, inc=1, **where(first, c))
    pl.semaphore_signal(barrier, inc=1, **where(last, c))
    pl.semaphore_signal(barrier, inc=1, **where(e, 1 - c))

    @pl.when(z < 3)
    def _():
        pl.semaphore_signal(barrier, inc=1, **where(up, c))

    @pl.when(z > 0)
    def _():
        pl.semaphore_signal(barrier, inc=1, **where(down, c))

    pl.semaphore_wait(barrier, 4 + (z + 1) // 2 % 2)
    for copy in loads:
        copy.wait()

    def gather_copy(t, j, kind, blk, core):
        target = (first, up, down, last, e)[kind]
        view = bufs[t][j].at[core, block(j, blk)]
        return pltpu.make_async_remote_copy(
            src_ref=view, dst_ref=view, send_sem=send.at[t * count + j, kind, blk],
            recv_sem=recv.at[t * count + j, kind // 4, blk], **where(target, 1 - c if kind == 4 else c))

    def arrive(t, j, blk):
        gather_copy(t, j, 0, blk, c).wait_recv()

    def each(t, j, blk, kinds, verb):
        for kind in kinds:
            do = getattr(gather_copy(t, j, kind, blk, c), verb)
            if kind == 1:
                pl.when(z < 3)(do)
            elif kind == 2:
                pl.when(z > 0)(do)
            else:
                do()

    def own(t, j):
        each(t, j, e, (0, 1, 2, 3, 4), "start")

    def first_step(t, j):
        blk = index(1 - a, b, z)
        arrive(t, j, blk)
        each(t, j, blk, (1, 2, 3, 4), "start")

    def z_step(t, j, k):
        for aa in (a, 1 - a):
            @pl.when(z >= k)
            def _():
                blk = index(aa, b, z - k)
                arrive(t, j, blk)
                each(t, j, blk, (1, 3, 4), "start")

            @pl.when(z + k <= 3)
            def _():
                blk = index(aa, b, z + k)
                arrive(t, j, blk)
                each(t, j, blk, (2, 3, 4), "start")

    def last_step(t, j, k):
        def over(blk):
            arrive(t, j, blk)
            each(t, j, blk, (4,), "start")

        for aa in (a, 1 - a):
            if k == 0:
                over(index(aa, 1 - b, z))
                continue

            @pl.when(z >= k)
            def _():
                over(index(aa, 1 - b, z - k))

            @pl.when(z + k <= 3)
            def _():
                over(index(aa, 1 - b, z + k))

    def sibling_step(t, j):
        @pl.loop(0, 16)
        def _(blk):
            gather_copy(t, j, 4, blk, 1 - c).wait_recv()

    def gather_sent(t, j):
        each(t, j, e, (0, 1, 2, 3, 4), "wait_send")
        each(t, j, index(1 - a, b, z), (1, 2, 3, 4), "wait_send")
        for k in range(1, 4):
            for aa in (a, 1 - a):
                pl.when(z >= k)(lambda: each(t, j, index(aa, b, z - k), (1, 3, 4), "wait_send"))
                pl.when(z + k <= 3)(lambda: each(t, j, index(aa, b, z + k), (2, 3, 4), "wait_send"))

        @pl.loop(0, 4)
        def _(zz):
            for aa in range(2):
                gather_copy(t, j, 4, index(aa, 1 - b, zz), c).wait_send()

    contract_last = (((1,), (1,)), ((), ()))

    def rows_of(j):
        return pl.ds(starts[j] * 16, sizes[j] * 16)

    def forward(j, lo, hi):
        @pl.loop(lo, hi)
        def _(i):
            cols = pl.ds(pl.multiple_of(i * 256, 256), 256)
            pre[:, cols] = lax.dot_general(
                xs[j][0], wgu[0, cols, :], contract_last, preferred_element_type=f32
            ) + lax.dot_general(xs[j][1], wgu[1, cols, :], contract_last, preferred_element_type=f32)

    def hidden_grad(j):
        hgrad[...] = lax.dot_general(
            ds_[j][0, :, pl.ds(0, half)], wd[0], contract_last, preferred_element_type=f32
        ) + lax.dot_general(ds_[j][1, :, pl.ds(0, half)], wd[1], contract_last, preferred_element_type=f32)

    def elementwise(j):
        @pl.loop(0, sizes[j] * 16 // 64)
        def _(i):
            here = pl.ds(pl.multiple_of(i * 64, 64), 64)
            lane = lax.broadcasted_iota(jnp.int32, (64, 128), 1)
            pieces = ds_[j][0, here, pl.ds(half, 128)].astype(f32)
            weight = jnp.sum(jnp.where(jnp.bitwise_and(lane, 15) == e, pieces, 0.0), axis=1, keepdims=True)
            gate_pre, up_pre = pre[here, pl.ds(0, hidden)], pre[here, pl.ds(hidden, hidden)]
            sigmoid = 1.0 / (1.0 + jnp.exp(-gate_pre))
            active = gate_pre * sigmoid
            grad = hgrad[here, :] * weight
            hid[here, :] = (active * up_pre * weight).astype(jnp.bfloat16)
            act[here, pl.ds(hidden, hidden)] = (grad * active).astype(jnp.bfloat16)
            act[here, pl.ds(0, hidden)] = (
                grad * up_pre * sigmoid * (1.0 + gate_pre * (1.0 - sigmoid))).astype(jnp.bfloat16)

    def transposed(j):
        act_t[:, rows_of(j)] = act[...].T
        hid_t[:, rows_of(j)] = hid[...].T

    def row_backward(j, side, dest):
        @pl.loop(0, half // 512)
        def _(i):
            cols = pl.ds(pl.multiple_of(i * 512, 512), 512)
            dest[:, cols] = jnp.dot(
                act[...], wgu[side, :, cols], preferred_element_type=f32).astype(jnp.bfloat16)

    def plane_of(q):
        swapped = (0, 1, 3, 2)[q]
        turn = q + ((z + 1) // 2 % 2) * (swapped - q)
        high = z // 2
        return high * turn + (1 - high) * (3 - turn)

    planes = [plane_of(q) for q in range(4)]

    def sibling_copy(j, zz):
        at = pl.ds(pl.multiple_of(zz * 4 * sizes[j], 16), 4 * sizes[j])
        return pltpu.make_async_remote_copy(
            src_ref=sib_out.at[at], dst_ref=sib_in[j].at[at], send_sem=sib_send.at[j, zz],
            recv_sem=sib_recv.at[j, zz], **where(e, 1 - c))

    def row_backward_out(j):
        if j > 0:
            for zz in planes:
                sibling_copy(j - 1, zz).wait_send()
        row_backward(j, 1 - c, sib_out)
        for zz in planes:
            sibling_copy(j, zz).start()

    def row_backward_own(j):
        row_backward(j, c, part[j])

    def add_rows(j, start, count, sources):
        dest = part[j]

        @pl.loop(0, count // 16)
        def _(i):
            here = pl.ds(pl.multiple_of(start + i * 16, 16), 16)
            total = dest[here, :].astype(f32)
            for ref, lead, offset in sources:
                there = pl.ds(pl.multiple_of(offset + i * 16, 16), 16)
                total = total + (ref[there, :] if lead is None else ref[lead, there, :]).astype(f32)
            dest[here, :] = total.astype(jnp.bfloat16)

    def last_copy(j, zz, aa):
        slot = zz * 2 + aa
        return pltpu.make_async_remote_copy(
            src_ref=part[j].at[block(j, index(aa, 1 - b, zz))], dst_ref=from_last[j].at[slot],
            send_sem=last_send.at[j, slot], recv_sem=last_recv.at[j, slot], **where(last, c))

    def z_copy(j, way, zz, aa):
        slot = (zz + 1 - way) * 2 + aa
        return pltpu.make_async_remote_copy(
            src_ref=part[j].at[block(j, index(aa, b, zz))], dst_ref=from_z[j].at[slot],
            send_sem=z_send.at[j, slot], recv_sem=z_recv.at[j, slot], **where(down if way else up, c))

    def reduce_last(j, q):
        zz = planes[q]
        sibling_copy(j, zz).wait_recv()
        for aa in range(2):
            start = index(aa, 1 - b, zz) * sizes[j]
            add_rows(j, start, sizes[j], [(sib_in[j], None, start)])
            last_copy(j, zz, aa).start()

    def reduce_z(j, q):
        zz, final = planes[q], q == 3
        for aa in range(2):
            start = index(aa, b, zz) * sizes[j]
            last_copy(j, zz, aa).wait_recv()
            add_rows(j, start, sizes[j], [(sib_in[j], None, start), (from_last[j], zz * 2 + aa, 0)])
            for way in range(2):
                reached = (z > 0) if way == 0 else (z < 3)
                ours = True if final else (zz > z if way == 0 else zz < z)

                @pl.when(jnp.logical_and(reached, ours))
                def _():
                    z_copy(j, way, zz, aa).wait_recv()
                    add_rows(j, start, sizes[j], [(from_z[j], (zz + 1 - way) * 2 + aa, 0)])

                if not final:
                    pl.when(ours)(z_copy(j, way, zz, aa).start)

    def first_copy(j):
        return pltpu.make_async_remote_copy(
            src_ref=part[j].at[block(j, first)], dst_ref=from_first[j], send_sem=first_send.at[j],
            recv_sem=first_recv.at[j], **where(first, c))

    def finish(j):
        first_copy(j).wait_recv()

        @pl.loop(0, sizes[j] // 16)
        def _(i):
            here = pl.ds(pl.multiple_of(i * 16, 16), 16)
            mine = pl.ds(pl.multiple_of(e * sizes[j] + i * 16, 16), 16)
            out_ref[pl.ds(pl.multiple_of(starts[j] + i * 16, 16), 16), :] = (
                part[j][mine, :].astype(f32) + from_first[j][here, :].astype(f32)).astype(jnp.bfloat16)

    outs = (gg_ref, gu_ref, gd_ref)

    def weight_copy(m, h):
        held = acc.at[h, pl.ds(m * hidden, hidden)] if m < 2 else wd.at[h]
        return pltpu.make_async_copy(held, outs[m].at[0, :, pl.ds(h * half, half)], out_sem.at[m, h])

    def weight_grad(m, h, chunks, more=False):
        lhs, rhs = (act_t, xs) if m < 2 else (hid_t, ds_)
        rows = pl.ds(m * hidden if m < 2 else 0, hidden)
        dest = acc if m < 2 else wd

        @pl.loop(0, half // 512)
        def _(i):
            cols = pl.ds(pl.multiple_of(i * 512, 512), 512)
            total = dest[h, rows, cols].astype(f32) if more else None
            for j in chunks:
                term = jnp.dot(lhs[rows, rows_of(j)], rhs[j][h, :, cols], preferred_element_type=f32)
                total = term if total is None else total + term
            dest[h, rows, cols] = total.astype(jnp.bfloat16)

    def weight_done(m, h, chunks, more=False):
        weight_grad(m, h, chunks, more)
        weight_copy(m, h).start()

    order = [(t, j) for j in range(count) for t in range(2)]

    def stage(n, work):
        tj = order[n]
        following = order[n + 1] if n + 1 < len(order) else None
        last_step(*tj, 0)
        z_step(*tj, 2)
        if following:
            own(*following)
        for do in work[0]:
            do()
        last_step(*tj, 1)
        z_step(*tj, 3)
        if following:
            first_step(*following)
        for do in work[1]:
            do()
        last_step(*tj, 2)
        if following:
            z_step(*following, 1)
        for do in work[2]:
            do()
        last_step(*tj, 3)
        for do in work[3]:
            do()
        sibling_step(*tj)

    def call(f, *args):
        return lambda: f(*args)

    own(0, 0)
    first_step(0, 0)
    z_step(0, 0, 1)
    stage(0, ((), (), (), ()))
    for copy in weights:
        copy.wait()
    stage(1, ([call(forward, 0, 0, 1)], [call(forward, 0, 1, 2)], [call(forward, 0, 2, 3)], ()))
    for j in range(2):
        stage(2 * j + 2, (
            [call(hidden_grad, j), call(elementwise, j)],
            [call(row_backward_out, j)],
            [call(row_backward_own, j)],
            ([call(reduce_z, j - 1, 3), call(first_copy(j - 1).start)] if j > 0 else [])
            + [call(reduce_last, j, 0), call(reduce_last, j, 1), call(transposed, j)],
        ))
        stage(2 * j + 3, (
            [call(forward, j + 1, 0, 1), call(reduce_last, j, 2), call(reduce_z, j, 0)],
            [call(forward, j + 1, 1, 2), call(reduce_last, j, 3)],
            [call(forward, j + 1, 2, 3), call(reduce_z, j, 1)],
            [call(weight_grad, 0, 0, (0, 1)), call(reduce_z, j, 2), call(weight_grad, 0, 1, (0, 1))]
            if j == 1 else [call(reduce_z, j, 2)],
        ))

    hidden_grad(2)
    elementwise(2)
    row_backward_out(2)
    row_backward_own(2)
    reduce_last(2, 0)
    reduce_last(2, 1)
    reduce_z(1, 3)
    first_copy(1).start()
    reduce_last(2, 2)
    reduce_z(2, 0)
    reduce_last(2, 3)
    transposed(2)
    weight_done(0, 0, (2,), True)
    reduce_z(2, 1)
    weight_done(0, 1, (2,), True)
    weight_done(1, 0, (0, 1, 2))
    reduce_z(2, 2)
    weight_done(1, 1, (0, 1, 2))
    finish(0)
    finish(1)
    reduce_z(2, 3)
    first_copy(2).start()
    weight_done(2, 0, (0, 1, 2))
    weight_done(2, 1, (0, 1, 2))
    finish(2)

    for m in range(3):
        for h in range(2):
            weight_copy(m, h).wait()
    for j in range(count):
        first_copy(j).wait_send()
        for q in range(4):
            zz = planes[q]
            if j == count - 1:
                sibling_copy(j, zz).wait_send()
            for aa in range(2):
                last_copy(j, zz, aa).wait_send()
                if q < 3:
                    pl.when(zz > z)(z_copy(j, 0, zz, aa).wait_send)
                    pl.when(zz < z)(z_copy(j, 1, zz, aa).wait_send)
        gather_sent(0, j)
        gather_sent(1, j)


def on_device_tree(tokens, cotangent, expert_ids, gate_values, w_gate, w_up, w_down):
    rows, half = tokens.shape
    hidden = w_gate.shape[1]
    experts = lax.axis_size("expert")
    total = rows * experts
    sizes = (rows // 3,) * 3
    chosen = expert_ids[:, :, None] == jnp.arange(experts, dtype=jnp.int32)[None, None, :]
    dense = jnp.sum(jnp.where(chosen, gate_values[:, :, None], 0.0), axis=1)
    high = lax.reduce_precision(dense, 8, 7)
    middle = lax.reduce_precision(dense - high, 8, 7)
    low = dense - high - middle
    gates = jnp.concatenate(
        [high, middle, low, jnp.zeros((rows, 128 - 3 * experts), jnp.float32)], axis=1).astype(jnp.bfloat16)
    bf16, f32 = jnp.bfloat16, jnp.float32
    any_, vmem = pl.BlockSpec(memory_space=pl.ANY), pl.BlockSpec(memory_space=pltpu.VMEM)
    dma = pltpu.SemaphoreType.DMA
    whole = tuple(size * experts for size in sizes)

    def chunks(*shape):
        return [pltpu.VMEM(tuple(n[j] if isinstance(n, tuple) else n for n in shape), bf16) for j in range(3)]

    return tuple(pl.pallas_call(
        functools.partial(merge_kernel, sizes),
        out_shape=(
            jax.ShapeDtypeStruct(tokens.shape, bf16),
            jax.ShapeDtypeStruct(w_gate.shape, bf16),
            jax.ShapeDtypeStruct(w_up.shape, bf16),
            jax.ShapeDtypeStruct(w_down.shape, bf16),
        ),
        in_specs=[any_, any_, vmem, any_, any_, any_],
        out_specs=(vmem, any_, any_, any_),
        scratch_shapes=[
            chunks(2, whole, half),
            chunks(2, whole, half + 128),
            pltpu.VMEM((2, 2 * hidden, half), bf16),
            pltpu.VMEM((2, hidden, half), bf16),
            pltpu.VMEM((whole[0], 2 * hidden), f32),
            pltpu.VMEM((whole[0], hidden), f32),
            pltpu.VMEM((whole[0], 2 * hidden), bf16),
            pltpu.VMEM((whole[0], hidden), bf16),
            pltpu.VMEM((2 * hidden, total), bf16),
            pltpu.VMEM((hidden, total), bf16),
            chunks(whole, half),
            pltpu.VMEM((whole[0], half), bf16),
            chunks(whole, half),
            chunks(8, sizes, half),
            chunks(10, sizes, half),
            chunks(sizes, half),
            pltpu.VMEM((2, 2 * hidden, half), bf16),
            dma((12,)),
            dma((6, 5, 16)),
            dma((6, 2, 16)),
            dma((3, 4)),
            dma((3, 4)),
            dma((3, 8)),
            dma((3, 8)),
            dma((3, 10)),
            dma((3, 10)),
            dma((3,)),
            dma((3,)),
            dma((3, 2)),
        ],
        compiler_params=pltpu.CompilerParams(
            collective_id=0, has_side_effects=True, vmem_limit_bytes=45 * 1024 * 1024),
        cost_estimate=pl.CostEstimate(
            flops=16 * total * hidden * 2 * half, bytes_accessed=24 * hidden * half, transcendentals=total * hidden),
    )(tokens, cotangent, gates, w_gate, w_up, w_down))


def solution(mesh):
    tree = mesh.shape["expert"] == 16 and mesh.shape["tensor"] == 2
    return jax.shard_map(
        on_device_tree if tree else on_device,
        mesh=mesh,
        in_specs=(
            P("expert", "tensor"),
            P("expert", "tensor"),
            P("expert", None),
            P("expert", None),
            P("expert", "tensor", None),
            P("expert", "tensor", None),
            P("expert", "tensor", None),
        ),
        out_specs=(
            P("expert", "tensor"),
            P("expert", "tensor", None),
            P("expert", "tensor", None),
            P("expert", "tensor", None),
        ),
        check_vma=False,
    )
```

```python
import functools

import jax
import jax.numpy as jnp
from jax import lax
from jax.experimental import pallas as pl
from jax.experimental.pallas import tpu as pltpu
from jax.sharding import PartitionSpec as P

TOP = 8
MESH = pl.DeviceIdType.MESH


def expert_backward(rows_x, rows_d, w_gate, w_up, w_down):
    gate_pre = jnp.einsum("secd,ehd->sech", rows_x, w_gate, preferred_element_type=jnp.float32)
    up_pre = jnp.einsum("secd,ehd->sech", rows_x, w_up, preferred_element_type=jnp.float32)
    sigmoid = jax.nn.sigmoid(gate_pre)
    active = gate_pre * sigmoid
    hidden = (active * up_pre).astype(jnp.bfloat16)
    hidden_grad = jnp.einsum("secd,ehd->sech", rows_d, w_down, preferred_element_type=jnp.float32)
    up_grad = (hidden_grad * active).astype(jnp.bfloat16)
    gate_grad = (hidden_grad * up_pre * sigmoid * (1.0 + gate_pre * (1.0 - sigmoid))).astype(
        jnp.bfloat16
    )
    grad_gate = jnp.einsum(
        "sech,secd->ehd", gate_grad, rows_x, preferred_element_type=jnp.float32
    ).astype(jnp.bfloat16)
    grad_up = jnp.einsum(
        "sech,secd->ehd", up_grad, rows_x, preferred_element_type=jnp.float32
    ).astype(jnp.bfloat16)
    grad_down = jnp.einsum(
        "sech,secd->ehd", hidden, rows_d, preferred_element_type=jnp.float32
    ).astype(jnp.bfloat16)
    partial_value = jnp.einsum(
        "sech,ehd->secd", gate_grad, w_gate, preferred_element_type=jnp.float32
    )
    partial_value = partial_value + jnp.einsum(
        "sech,ehd->secd", up_grad, w_up, preferred_element_type=jnp.float32
    )
    return (partial_value, grad_gate, grad_up, grad_down)


def on_device(tokens, cotangent, expert_ids, gate_values, w_gate, w_up, w_down):
    tok_count = expert_ids.shape[0]
    local_count = w_gate.shape[0]
    groups = lax.axis_size("expert")
    experts = local_count * groups
    capacity = 4 * tok_count * TOP // (3 * experts)
    feat_width = tokens.shape[1]
    flat_ids = expert_ids.reshape(-1)
    onehot = (flat_ids[:, None] == jnp.arange(experts, dtype=jnp.int32)[None, :]).astype(jnp.int32)
    before = jnp.cumsum(onehot, axis=0) - onehot
    slot_pos = jnp.sum(before * onehot, axis=1)
    target = flat_ids * capacity + slot_pos
    matches = (target[None, :] == jnp.arange(experts * capacity, dtype=jnp.int32)[:, None]).reshape(
        experts * capacity, tok_count, TOP
    )
    by_token = jnp.any(matches, axis=2)
    occupied = jnp.any(by_token, axis=1)
    token_iota = jnp.arange(tok_count, dtype=jnp.int32)
    owner = jnp.sum(jnp.where(by_token, token_iota[None, :], 0), axis=1)
    slot_weight = jnp.sum(jnp.sum(jnp.where(matches, gate_values[None, :, :], 0.0), axis=2), axis=1)
    full_x, full_d = (
        lax.all_gather(tokens, "tensor", axis=1, tiled=True),
        lax.all_gather(cotangent, "tensor", axis=1, tiled=True),
    )
    sent_x = jnp.where(occupied[:, None], full_x[owner], jnp.zeros((), jnp.bfloat16))
    sent_d = (slot_weight[:, None] * full_d[owner].astype(jnp.float32)).astype(jnp.bfloat16)
    buffer_shape = (groups, local_count, capacity, full_x.shape[1])
    sent_x, sent_d = (sent_x.reshape(buffer_shape), sent_d.reshape(buffer_shape))
    rows_x, rows_d = (
        lax.all_to_all(sent_x, "expert", split_axis=0, concat_axis=0, tiled=True),
        lax.all_to_all(sent_d, "expert", split_axis=0, concat_axis=0, tiled=True),
    )
    partial_value, grad_gate, grad_up, grad_down = expert_backward(
        rows_x, rows_d, w_gate, w_up, w_down
    )
    summed = lax.psum(partial_value.astype(jnp.bfloat16), "tensor").astype(jnp.float32)
    returned = lax.dynamic_slice_in_dim(
        summed, lax.axis_index("tensor") * feat_width, feat_width, 3
    ).astype(jnp.bfloat16)
    arrived = lax.all_to_all(returned, "expert", split_axis=0, concat_axis=0, tiled=True).reshape(
        experts * capacity, feat_width
    )
    masked = jnp.where(occupied[:, None], arrived.astype(jnp.float32), jnp.zeros((), jnp.float32))
    grad_tokens = jax.ops.segment_sum(masked, owner, num_segments=tok_count).astype(jnp.bfloat16)
    return (grad_tokens, grad_gate, grad_up, grad_down)


def merge_kernel(
    sizes, tok_ref, cot_ref, gate_ref, wg_ref, wu_ref, wd_ref,
    out_ref, gg_ref, gu_ref, gd_ref,
    xs, ds_, wgu, wd, pre, hgrad, act, hid, act_t, hid_t, part, sib_out, sib_in, from_last, from_z, from_first,
    load_sem, send, recv, across_send, across_recv, sib_send, sib_recv, last_send, last_recv, z_send, z_recv, first_send, first_recv, out_sem,
):
    half = tok_ref.shape[1]
    hidden = wg_ref.shape[1]
    f32 = jnp.float32
    starts = (0, sizes[0])
    e, c = lax.axis_index("expert"), lax.axis_index("tensor")
    x, y, z = e % 2, (e // 2) % 2, e // 4
    a, b = x + c * (y - x), y + c * (x - y)

    def index(aa, bb, zz):
        return zz * 4 + aa * (1 + c) + bb * (2 - c)

    def where(expert, core):
        return dict(device_id={"expert": expert, "tensor": core}, device_id_type=MESH)

    first, last = index(1 - a, b, z), index(a, 1 - b, z)
    up, down = e + 4, e - 4
    bufs = (xs, ds_)

    def block(j, blk):
        return pl.ds(pl.multiple_of(blk * sizes[j], 16), sizes[j])

    loads = []
    for t, ref in enumerate((tok_ref, cot_ref)):
        for j in range(2):
            loads.append(pltpu.make_async_copy(
                ref.at[pl.ds(starts[j], sizes[j])],
                bufs[t][j].at[c, block(j, e), pl.ds(0, half)], load_sem.at[t * 2 + j]))
    n = 4
    weights = []
    for h in range(2):
        cols = pl.ds(h * half, half)
        weights.append(pltpu.make_async_copy(wg_ref.at[0, :, cols], wgu.at[h, pl.ds(0, hidden)], load_sem.at[n]))
        weights.append(pltpu.make_async_copy(wu_ref.at[0, :, cols], wgu.at[h, pl.ds(hidden, hidden)], load_sem.at[n + 1]))
        weights.append(pltpu.make_async_copy(wd_ref.at[0, :, cols], wd.at[h], load_sem.at[n + 2]))
        n += 3
    for copy in loads + weights:
        copy.start()
    for j in range(2):
        ds_[j][c, block(j, e), half:] = gate_ref[starts[j]:starts[j] + sizes[j], :]

    barrier = pltpu.get_barrier_semaphore()
    pl.semaphore_signal(barrier, inc=1, **where(first, c))
    pl.semaphore_signal(barrier, inc=1, **where(last, c))
    pl.semaphore_signal(barrier, inc=1, **where(e, 1 - c))

    @pl.when(z < 3)
    def _():
        pl.semaphore_signal(barrier, inc=1, **where(up, c))

    @pl.when(z > 0)
    def _():
        pl.semaphore_signal(barrier, inc=1, **where(down, c))

    pl.semaphore_wait(barrier, 4 + (z + 1) // 2 % 2)
    for copy in loads:
        copy.wait()

    def gather_copy(t, j, kind, blk):
        view = bufs[t][j].at[c, block(j, blk)]
        return pltpu.make_async_remote_copy(
            src_ref=view, dst_ref=view, send_sem=send.at[t * 2 + j, kind, 0 if kind == 3 else blk],
            recv_sem=recv.at[t * 2 + j, blk], **where((first, up, down, last)[kind], c))

    def across(t, j, view):
        return pltpu.make_async_remote_copy(
            src_ref=view, dst_ref=view, send_sem=across_send.at[t * 2 + j],
            recv_sem=across_recv.at[t * 2 + j], **where(e, 1 - c))

    def plane(t, j, zz):
        across(t, j, bufs[t][j].at[c, pl.ds(pl.multiple_of(zz * 4 * sizes[j], 16), 4 * sizes[j])]).start()

    def arrive(t, j, blk):
        gather_copy(t, j, 0, blk).wait_recv()

    def each(t, j, blk, kinds, verb):
        for kind in kinds:
            do = getattr(gather_copy(t, j, kind, blk), verb)
            if kind == 1:
                pl.when(z < 3)(do)
            elif kind == 2:
                pl.when(z > 0)(do)
            else:
                do()

    def own(t, j):
        each(t, j, e, (0, 1, 2, 3), "start")

    def first_step(t, j):
        blk = index(1 - a, b, z)
        arrive(t, j, blk)
        each(t, j, blk, (1, 2, 3), "start")

    def z_step(t, j, k):
        for aa in (a, 1 - a):
            @pl.when(z >= k)
            def _():
                blk = index(aa, b, z - k)
                arrive(t, j, blk)
                each(t, j, blk, (1, 3), "start")

            @pl.when(z + k <= 3)
            def _():
                blk = index(aa, b, z + k)
                arrive(t, j, blk)
                each(t, j, blk, (2, 3), "start")

    def last_step(t, j, k):
        def over(zz):
            for aa in (a, 1 - a):
                arrive(t, j, index(aa, 1 - b, zz))
            plane(t, j, zz)

        if k == 0:
            over(z)
        else:
            pl.when(z >= k)(lambda: over(z - k))
            pl.when(z + k <= 3)(lambda: over(z + k))

    def sibling_step(t, j):
        across(t, j, bufs[t][j].at[1 - c]).wait_recv()

    def gather_sent(t, j):
        each(t, j, e, (0, 1, 2), "wait_send")
        each(t, j, index(1 - a, b, z), (1, 2), "wait_send")
        for k in range(1, 4):
            for aa in (a, 1 - a):
                pl.when(z >= k)(lambda: each(t, j, index(aa, b, z - k), (1,), "wait_send"))
                pl.when(z + k <= 3)(lambda: each(t, j, index(aa, b, z + k), (2,), "wait_send"))
        eight = bufs[t][j].at[c, pl.ds(0, 8 * sizes[j])]
        pltpu.make_async_remote_copy(
            src_ref=eight, dst_ref=eight, send_sem=send.at[t * 2 + j, 3, 0], recv_sem=recv.at[t * 2 + j, 0],
            **where(last, c)).wait_send()
        across(t, j, bufs[t][j].at[c]).wait_send()

    contract_last = (((1,), (1,)), ((), ()))

    def rows_of(j):
        return pl.ds(starts[j] * 16, sizes[j] * 16)

    def forward(j, lo, hi):
        @pl.loop(lo, hi)
        def _(i):
            cols = pl.ds(pl.multiple_of(i * 256, 256), 256)
            pre[pl.ds(0, sizes[j] * 16), cols] = lax.dot_general(
                xs[j][0], wgu[0, cols, :], contract_last, preferred_element_type=f32
            ) + lax.dot_general(xs[j][1], wgu[1, cols, :], contract_last, preferred_element_type=f32)

    def hidden_backward(j):
        @pl.loop(0, sizes[j] * 16 // 256)
        def _(i):
            at = pl.ds(pl.multiple_of(i * 256, 256), 256)
            hgrad[at, :] = lax.dot_general(
                ds_[j][0, at, pl.ds(0, half)], wd[0], contract_last, preferred_element_type=f32
            ) + lax.dot_general(ds_[j][1, at, pl.ds(0, half)], wd[1], contract_last, preferred_element_type=f32)

        @pl.loop(0, sizes[j] * 16 // 64)
        def _(i):
            there = pl.ds(pl.multiple_of(i * 64, 64), 64)
            here = pl.ds(pl.multiple_of(starts[j] * 16 + i * 64, 64), 64)
            lane = lax.broadcasted_iota(jnp.int32, (64, 128), 1)
            pieces = ds_[j][0, there, pl.ds(half, 128)].astype(f32)
            weight = jnp.sum(jnp.where(jnp.bitwise_and(lane, 15) == e, pieces, 0.0), axis=1, keepdims=True)
            gate_pre, up_pre = pre[there, pl.ds(0, hidden)], pre[there, pl.ds(hidden, hidden)]
            sigmoid = 1.0 / (1.0 + jnp.exp(-gate_pre))
            active = gate_pre * sigmoid
            grad = hgrad[there, :] * weight
            hid[here, :] = (active * up_pre * weight).astype(jnp.bfloat16)
            act[here, pl.ds(hidden, hidden)] = (grad * active).astype(jnp.bfloat16)
            act[here, pl.ds(0, hidden)] = (
                grad * up_pre * sigmoid * (1.0 + gate_pre * (1.0 - sigmoid))).astype(jnp.bfloat16)

    def row_backward(j, side, dest):
        @pl.loop(0, half // 512)
        def _(i):
            cols = pl.ds(pl.multiple_of(i * 512, 512), 512)
            dest[j][:, cols] = jnp.dot(
                act[rows_of(j), :], wgu[side, :, cols], preferred_element_type=f32).astype(jnp.bfloat16)

    def plane_of(q):
        swapped = (0, 1, 3, 2)[q]
        turn = q + ((z + 1) // 2 % 2) * (swapped - q)
        high = z // 2
        return high * turn + (1 - high) * (3 - turn)

    planes = [plane_of(q) for q in range(4)]

    def sibling_copy(j, zz):
        at = pl.ds(pl.multiple_of(zz * 4 * sizes[j], 16), 4 * sizes[j])
        return pltpu.make_async_remote_copy(
            src_ref=sib_out[j].at[at], dst_ref=sib_in[j].at[at], send_sem=sib_send.at[j, zz],
            recv_sem=sib_recv.at[j, zz], **where(e, 1 - c))

    def row_backward_out(j):
        row_backward(j, 1 - c, sib_out)
        for zz in planes:
            sibling_copy(j, zz).start()

    def row_backward_own(j):
        row_backward(j, c, part)

    def add_rows(j, start, count, sources):
        dest = part[j]

        @pl.loop(0, count // 16)
        def _(i):
            here = pl.ds(pl.multiple_of(start + i * 16, 16), 16)
            total = dest[here, :].astype(f32)
            for ref, lead, offset in sources:
                there = pl.ds(pl.multiple_of(offset + i * 16, 16), 16)
                total = total + (ref[there, :] if lead is None else ref[lead, there, :]).astype(f32)
            dest[here, :] = total.astype(jnp.bfloat16)

    def last_copy(j, zz, aa):
        slot = zz * 2 + aa
        return pltpu.make_async_remote_copy(
            src_ref=part[j].at[block(j, index(aa, 1 - b, zz))], dst_ref=from_last[j].at[slot],
            send_sem=last_send.at[j, slot], recv_sem=last_recv.at[j, slot], **where(last, c))

    def z_copy(j, way, zz, aa):
        slot = (zz + 1 - way) * 2 + aa
        return pltpu.make_async_remote_copy(
            src_ref=part[j].at[block(j, index(aa, b, zz))], dst_ref=from_z[j].at[slot],
            send_sem=z_send.at[j, slot], recv_sem=z_recv.at[j, slot], **where(down if way else up, c))

    def reduce_last(j, q):
        zz = planes[q]
        sibling_copy(j, zz).wait_recv()
        for aa in range(2):
            start = index(aa, 1 - b, zz) * sizes[j]
            add_rows(j, start, sizes[j], [(sib_in[j], None, start)])
            last_copy(j, zz, aa).start()

    def reduce_z(j, q):
        zz, final = planes[q], q == 3
        for aa in range(2):
            start = index(aa, b, zz) * sizes[j]
            last_copy(j, zz, aa).wait_recv()
            add_rows(j, start, sizes[j], [(sib_in[j], None, start), (from_last[j], zz * 2 + aa, 0)])
            for way in range(2):
                reached = (z > 0) if way == 0 else (z < 3)
                ours = True if final else (zz > z if way == 0 else zz < z)

                @pl.when(jnp.logical_and(reached, ours))
                def _():
                    z_copy(j, way, zz, aa).wait_recv()
                    add_rows(j, start, sizes[j], [(from_z[j], (zz + 1 - way) * 2 + aa, 0)])

                if not final:
                    pl.when(ours)(z_copy(j, way, zz, aa).start)

    def first_copy(j):
        return pltpu.make_async_remote_copy(
            src_ref=part[j].at[block(j, first)], dst_ref=from_first[j], send_sem=first_send.at[j],
            recv_sem=first_recv.at[j], **where(first, c))

    def finish(j):
        first_copy(j).wait_recv()

        @pl.loop(0, sizes[j] // 16)
        def _(i):
            here = pl.ds(pl.multiple_of(i * 16, 16), 16)
            mine = pl.ds(pl.multiple_of(e * sizes[j] + i * 16, 16), 16)
            out_ref[pl.ds(pl.multiple_of(starts[j] + i * 16, 16), 16), :] = (
                part[j][mine, :].astype(f32) + from_first[j][here, :].astype(f32)).astype(jnp.bfloat16)

    outs = (gg_ref, gu_ref, gd_ref)

    def weight_copy(m, h):
        held = wgu.at[h, pl.ds(m * hidden, hidden)] if m < 2 else wd.at[h]
        return pltpu.make_async_copy(held, outs[m].at[0, :, pl.ds(h * half, half)], out_sem.at[m, h])

    def weight_grad(m, h):
        lhs, rhs = (act_t, xs) if m < 2 else (hid_t, ds_)
        base = m * hidden if m < 2 else 0

        @pl.loop(0, half // 512)
        def _(i):
            cols = pl.ds(pl.multiple_of(i * 512, 512), 512)
            total = jnp.dot(
                lhs[pl.ds(base, hidden), rows_of(0)], rhs[0][h, :, cols], preferred_element_type=f32
            ) + jnp.dot(lhs[pl.ds(base, hidden), rows_of(1)], rhs[1][h, :, cols], preferred_element_type=f32)
            if m < 2:
                wgu[h, pl.ds(base, hidden), cols] = total.astype(jnp.bfloat16)
            else:
                wd[h, :, cols] = total.astype(jnp.bfloat16)

        weight_copy(m, h).start()

    X, G = 0, 1
    own(X, 0)
    first_step(X, 0)
    z_step(X, 0, 1)
    own(G, 0)
    last_step(X, 0, 0)
    z_step(X, 0, 2)
    last_step(X, 0, 1)
    z_step(X, 0, 3)
    first_step(G, 0)
    own(X, 1)
    last_step(X, 0, 2)
    z_step(G, 0, 1)
    last_step(X, 0, 3)
    for copy in weights:
        copy.wait()
    last_step(G, 0, 0)
    z_step(G, 0, 2)
    sibling_step(X, 0)
    forward(0, 0, 1)
    last_step(G, 0, 1)
    z_step(G, 0, 3)
    first_step(X, 1)
    own(G, 1)
    forward(0, 1, 2)
    last_step(G, 0, 2)
    z_step(X, 1, 1)
    forward(0, 2, 3)
    last_step(G, 0, 3)
    last_step(X, 1, 0)
    sibling_step(G, 0)

    hidden_backward(0)
    z_step(X, 1, 2)
    last_step(X, 1, 1)
    first_step(G, 1)
    row_backward_out(0)
    z_step(X, 1, 3)
    last_step(X, 1, 2)
    z_step(G, 1, 1)
    row_backward_own(0)
    last_step(X, 1, 3)
    last_step(G, 1, 0)
    reduce_last(0, 0)
    reduce_last(0, 1)
    z_step(G, 1, 2)
    reduce_z(0, 0)
    reduce_last(0, 2)
    sibling_step(X, 1)
    last_step(G, 1, 1)
    forward(1, 0, 1)
    z_step(G, 1, 3)
    reduce_z(0, 1)
    reduce_last(0, 3)
    forward(1, 1, 2)
    last_step(G, 1, 2)
    reduce_z(0, 2)
    forward(1, 2, 3)
    last_step(G, 1, 3)
    reduce_z(0, 3)
    first_copy(0).start()
    sibling_step(G, 1)

    hidden_backward(1)
    row_backward_out(1)
    row_backward_own(1)
    reduce_last(1, 0)
    reduce_last(1, 1)
    reduce_last(1, 2)
    reduce_z(1, 0)
    reduce_last(1, 3)
    act_t[...] = act[...].T
    weight_grad(0, 0)
    reduce_z(1, 1)
    weight_grad(0, 1)
    weight_grad(1, 0)
    reduce_z(1, 2)
    weight_grad(1, 1)
    finish(0)
    hid_t[...] = hid[...].T
    reduce_z(1, 3)
    first_copy(1).start()
    weight_grad(2, 0)
    weight_grad(2, 1)
    finish(1)

    for m in range(3):
        for h in range(2):
            weight_copy(m, h).wait()
    for j in range(2):
        first_copy(j).wait_send()
        for q in range(4):
            zz = planes[q]
            sibling_copy(j, zz).wait_send()
            for aa in range(2):
                last_copy(j, zz, aa).wait_send()
                if q < 3:
                    pl.when(zz > z)(z_copy(j, 0, zz, aa).wait_send)
                    pl.when(zz < z)(z_copy(j, 1, zz, aa).wait_send)
        gather_sent(0, j)
        gather_sent(1, j)


def on_device_tree(tokens, cotangent, expert_ids, gate_values, w_gate, w_up, w_down):
    rows, half = tokens.shape
    hidden = w_gate.shape[1]
    experts = lax.axis_size("expert")
    total = rows * experts
    sizes = (rows // 48 * 16, rows // 48 * 32)
    chosen = expert_ids[:, :, None] == jnp.arange(experts, dtype=jnp.int32)[None, None, :]
    dense = jnp.sum(jnp.where(chosen, gate_values[:, :, None], 0.0), axis=1)
    high = lax.reduce_precision(dense, 8, 7)
    middle = lax.reduce_precision(dense - high, 8, 7)
    low = dense - high - middle
    gates = jnp.concatenate(
        [high, middle, low, jnp.zeros((rows, 128 - 3 * experts), jnp.float32)], axis=1).astype(jnp.bfloat16)
    bf16, f32 = jnp.bfloat16, jnp.float32
    any_, vmem = pl.BlockSpec(memory_space=pl.ANY), pl.BlockSpec(memory_space=pltpu.VMEM)
    dma = pltpu.SemaphoreType.DMA
    whole = tuple(size * experts for size in sizes)

    def chunks(*shape):
        return [pltpu.VMEM(tuple(n[j] if isinstance(n, tuple) else n for n in shape), bf16) for j in range(2)]

    return tuple(pl.pallas_call(
        functools.partial(merge_kernel, sizes),
        out_shape=(
            jax.ShapeDtypeStruct(tokens.shape, bf16),
            jax.ShapeDtypeStruct(w_gate.shape, bf16),
            jax.ShapeDtypeStruct(w_up.shape, bf16),
            jax.ShapeDtypeStruct(w_down.shape, bf16),
        ),
        in_specs=[any_, any_, vmem, any_, any_, any_],
        out_specs=(vmem, any_, any_, any_),
        scratch_shapes=[
            chunks(2, whole, half),
            chunks(2, whole, half + 128),
            pltpu.VMEM((2, 2 * hidden, half), bf16),
            pltpu.VMEM((2, hidden, half), bf16),
            pltpu.VMEM((whole[1], 2 * hidden), f32),
            pltpu.VMEM((whole[1], hidden), f32),
            pltpu.VMEM((total, 2 * hidden), bf16),
            pltpu.VMEM((total, hidden), bf16),
            pltpu.VMEM((2 * hidden, total), bf16),
            pltpu.VMEM((hidden, total), bf16),
            chunks(whole, half),
            chunks(whole, half),
            chunks(whole, half),
            chunks(8, sizes, half),
            chunks(10, sizes, half),
            chunks(sizes, half),
            dma((10,)),
            dma((4, 4, 16)),
            dma((4, 16)),
            dma((4,)),
            dma((4,)),
            dma((2, 4)),
            dma((2, 4)),
            dma((2, 8)),
            dma((2, 8)),
            dma((2, 10)),
            dma((2, 10)),
            dma((2,)),
            dma((2,)),
            dma((3, 2)),
        ],
        compiler_params=pltpu.CompilerParams(
            collective_id=0, has_side_effects=True, vmem_limit_bytes=43 * 1024 * 1024),
        cost_estimate=pl.CostEstimate(
            flops=16 * total * hidden * 2 * half, bytes_accessed=24 * hidden * half, transcendentals=total * hidden),
    )(tokens, cotangent, gates, w_gate, w_up, w_down))


def solution(mesh):
    tree = mesh.shape["expert"] == 16 and mesh.shape["tensor"] == 2
    return jax.shard_map(
        on_device_tree if tree else on_device,
        mesh=mesh,
        in_specs=(
            P("expert", "tensor"),
            P("expert", "tensor"),
            P("expert", None),
            P("expert", None),
            P("expert", "tensor", None),
            P("expert", "tensor", None),
            P("expert", "tensor", None),
        ),
        out_specs=(
            P("expert", "tensor"),
            P("expert", "tensor", None),
            P("expert", "tensor", None),
            P("expert", "tensor", None),
        ),
        check_vma=False,
    )
```

```python
import functools

import jax
import jax.numpy as jnp
from jax import lax
from jax.experimental import pallas as pl
from jax.experimental.pallas import tpu as pltpu
from jax.sharding import PartitionSpec as P

TOP = 8
MESH = pl.DeviceIdType.MESH


def expert_backward(rows_x, rows_d, w_gate, w_up, w_down):
    gate_pre = jnp.einsum("secd,ehd->sech", rows_x, w_gate, preferred_element_type=jnp.float32)
    up_pre = jnp.einsum("secd,ehd->sech", rows_x, w_up, preferred_element_type=jnp.float32)
    sigmoid = jax.nn.sigmoid(gate_pre)
    active = gate_pre * sigmoid
    hidden = (active * up_pre).astype(jnp.bfloat16)
    hidden_grad = jnp.einsum("secd,ehd->sech", rows_d, w_down, preferred_element_type=jnp.float32)
    up_grad = (hidden_grad * active).astype(jnp.bfloat16)
    gate_grad = (hidden_grad * up_pre * sigmoid * (1.0 + gate_pre * (1.0 - sigmoid))).astype(
        jnp.bfloat16
    )
    grad_gate = jnp.einsum(
        "sech,secd->ehd", gate_grad, rows_x, preferred_element_type=jnp.float32
    ).astype(jnp.bfloat16)
    grad_up = jnp.einsum(
        "sech,secd->ehd", up_grad, rows_x, preferred_element_type=jnp.float32
    ).astype(jnp.bfloat16)
    grad_down = jnp.einsum(
        "sech,secd->ehd", hidden, rows_d, preferred_element_type=jnp.float32
    ).astype(jnp.bfloat16)
    partial_value = jnp.einsum(
        "sech,ehd->secd", gate_grad, w_gate, preferred_element_type=jnp.float32
    )
    partial_value = partial_value + jnp.einsum(
        "sech,ehd->secd", up_grad, w_up, preferred_element_type=jnp.float32
    )
    return (partial_value, grad_gate, grad_up, grad_down)


def on_device(tokens, cotangent, expert_ids, gate_values, w_gate, w_up, w_down):
    tok_count = expert_ids.shape[0]
    local_count = w_gate.shape[0]
    groups = lax.axis_size("expert")
    experts = local_count * groups
    capacity = 4 * tok_count * TOP // (3 * experts)
    feat_width = tokens.shape[1]
    flat_ids = expert_ids.reshape(-1)
    onehot = (flat_ids[:, None] == jnp.arange(experts, dtype=jnp.int32)[None, :]).astype(jnp.int32)
    before = jnp.cumsum(onehot, axis=0) - onehot
    slot_pos = jnp.sum(before * onehot, axis=1)
    target = flat_ids * capacity + slot_pos
    matches = (target[None, :] == jnp.arange(experts * capacity, dtype=jnp.int32)[:, None]).reshape(
        experts * capacity, tok_count, TOP
    )
    by_token = jnp.any(matches, axis=2)
    occupied = jnp.any(by_token, axis=1)
    token_iota = jnp.arange(tok_count, dtype=jnp.int32)
    owner = jnp.sum(jnp.where(by_token, token_iota[None, :], 0), axis=1)
    slot_weight = jnp.sum(jnp.sum(jnp.where(matches, gate_values[None, :, :], 0.0), axis=2), axis=1)
    full_x, full_d = (
        lax.all_gather(tokens, "tensor", axis=1, tiled=True),
        lax.all_gather(cotangent, "tensor", axis=1, tiled=True),
    )
    sent_x = jnp.where(occupied[:, None], full_x[owner], jnp.zeros((), jnp.bfloat16))
    sent_d = (slot_weight[:, None] * full_d[owner].astype(jnp.float32)).astype(jnp.bfloat16)
    buffer_shape = (groups, local_count, capacity, full_x.shape[1])
    sent_x, sent_d = (sent_x.reshape(buffer_shape), sent_d.reshape(buffer_shape))
    rows_x, rows_d = (
        lax.all_to_all(sent_x, "expert", split_axis=0, concat_axis=0, tiled=True),
        lax.all_to_all(sent_d, "expert", split_axis=0, concat_axis=0, tiled=True),
    )
    partial_value, grad_gate, grad_up, grad_down = expert_backward(
        rows_x, rows_d, w_gate, w_up, w_down
    )
    summed = lax.psum(partial_value.astype(jnp.bfloat16), "tensor").astype(jnp.float32)
    returned = lax.dynamic_slice_in_dim(
        summed, lax.axis_index("tensor") * feat_width, feat_width, 3
    ).astype(jnp.bfloat16)
    arrived = lax.all_to_all(returned, "expert", split_axis=0, concat_axis=0, tiled=True).reshape(
        experts * capacity, feat_width
    )
    masked = jnp.where(occupied[:, None], arrived.astype(jnp.float32), jnp.zeros((), jnp.float32))
    grad_tokens = jax.ops.segment_sum(masked, owner, num_segments=tok_count).astype(jnp.bfloat16)
    return (grad_tokens, grad_gate, grad_up, grad_down)


def merge_kernel(
    sizes, tok_ref, cot_ref, gate_ref, wg_ref, wu_ref, wd_ref,
    out_ref, gg_ref, gu_ref, gd_ref,
    xs, ds_, wgu, wd, pre, hgrad, act, hid, act_t, hid_t, part, sib_out, sib_in, from_last, from_z, from_first,
    load_sem, send, recv, across_send, across_recv, sib_send, sib_recv, last_send, last_recv, z_send, z_recv, first_send, first_recv, out_sem,
):
    half = tok_ref.shape[1]
    hidden = wg_ref.shape[1]
    f32 = jnp.float32
    starts = (0, sizes[0])
    e, c = lax.axis_index("expert"), lax.axis_index("tensor")
    x, y, z = e % 2, (e // 2) % 2, e // 4
    a, b = x + c * (y - x), y + c * (x - y)

    def index(aa, bb, zz):
        return zz * 4 + aa * (1 + c) + bb * (2 - c)

    def where(expert, core):
        return dict(device_id={"expert": expert, "tensor": core}, device_id_type=MESH)

    first, last = index(1 - a, b, z), index(a, 1 - b, z)
    up, down = e + 4, e - 4
    bufs = (xs, ds_)

    def block(j, blk):
        return pl.ds(pl.multiple_of(blk * sizes[j], 16), sizes[j])

    loads = []
    for t, ref in enumerate((tok_ref, cot_ref)):
        for j in range(2):
            loads.append(pltpu.make_async_copy(
                ref.at[pl.ds(starts[j], sizes[j])],
                bufs[t][j].at[c, block(j, e), pl.ds(0, half)], load_sem.at[t * 2 + j]))
    n = 4
    weights = []
    for h in range(2):
        cols = pl.ds(h * half, half)
        weights.append(pltpu.make_async_copy(wg_ref.at[0, :, cols], wgu.at[h, pl.ds(0, hidden)], load_sem.at[n]))
        weights.append(pltpu.make_async_copy(wu_ref.at[0, :, cols], wgu.at[h, pl.ds(hidden, hidden)], load_sem.at[n + 1]))
        weights.append(pltpu.make_async_copy(wd_ref.at[0, :, cols], wd.at[h], load_sem.at[n + 2]))
        n += 3
    for copy in loads + weights:
        copy.start()
    for j in range(2):
        ds_[j][c, block(j, e), half:] = gate_ref[starts[j]:starts[j] + sizes[j], :]

    barrier = pltpu.get_barrier_semaphore()
    pl.semaphore_signal(barrier, inc=1, **where(first, c))
    pl.semaphore_signal(barrier, inc=1, **where(last, c))
    pl.semaphore_signal(barrier, inc=1, **where(e, 1 - c))

    @pl.when(z < 3)
    def _():
        pl.semaphore_signal(barrier, inc=1, **where(up, c))

    @pl.when(z > 0)
    def _():
        pl.semaphore_signal(barrier, inc=1, **where(down, c))

    pl.semaphore_wait(barrier, 4 + (z + 1) // 2 % 2)
    for copy in loads:
        copy.wait()

    def gather_copy(t, j, kind, blk):
        view = bufs[t][j].at[c, block(j, blk)]
        return pltpu.make_async_remote_copy(
            src_ref=view, dst_ref=view, send_sem=send.at[t * 2 + j, kind, 0 if kind == 3 else blk],
            recv_sem=recv.at[t * 2 + j, blk], **where((first, up, down, last)[kind], c))

    def across(t, j, view):
        return pltpu.make_async_remote_copy(
            src_ref=view, dst_ref=view, send_sem=across_send.at[t * 2 + j],
            recv_sem=across_recv.at[t * 2 + j], **where(e, 1 - c))

    def plane(t, j, zz):
        across(t, j, bufs[t][j].at[c, pl.ds(pl.multiple_of(zz * 4 * sizes[j], 16), 4 * sizes[j])]).start()

    def arrive(t, j, blk):
        gather_copy(t, j, 0, blk).wait_recv()

    def each(t, j, blk, kinds, verb):
        for kind in kinds:
            do = getattr(gather_copy(t, j, kind, blk), verb)
            if kind == 1:
                pl.when(z < 3)(do)
            elif kind == 2:
                pl.when(z > 0)(do)
            else:
                do()

    def own(t, j):
        each(t, j, e, (0, 1, 2, 3), "start")

    def first_step(t, j):
        blk = index(1 - a, b, z)
        arrive(t, j, blk)
        each(t, j, blk, (1, 2, 3), "start")

    def z_step(t, j, k):
        for aa in (a, 1 - a):
            @pl.when(z >= k)
            def _():
                blk = index(aa, b, z - k)
                arrive(t, j, blk)
                each(t, j, blk, (1, 3), "start")

            @pl.when(z + k <= 3)
            def _():
                blk = index(aa, b, z + k)
                arrive(t, j, blk)
                each(t, j, blk, (2, 3), "start")

    def last_step(t, j, k):
        def over(zz):
            for aa in (a, 1 - a):
                arrive(t, j, index(aa, 1 - b, zz))
            plane(t, j, zz)

        if k == 0:
            over(z)
        else:
            pl.when(z >= k)(lambda: over(z - k))
            pl.when(z + k <= 3)(lambda: over(z + k))

    def sibling_step(t, j):
        across(t, j, bufs[t][j].at[1 - c]).wait_recv()

    def gather_sent(t, j):
        each(t, j, e, (0, 1, 2), "wait_send")
        each(t, j, index(1 - a, b, z), (1, 2), "wait_send")
        for k in range(1, 4):
            for aa in (a, 1 - a):
                pl.when(z >= k)(lambda: each(t, j, index(aa, b, z - k), (1,), "wait_send"))
                pl.when(z + k <= 3)(lambda: each(t, j, index(aa, b, z + k), (2,), "wait_send"))
        eight = bufs[t][j].at[c, pl.ds(0, 8 * sizes[j])]
        pltpu.make_async_remote_copy(
            src_ref=eight, dst_ref=eight, send_sem=send.at[t * 2 + j, 3, 0], recv_sem=recv.at[t * 2 + j, 0],
            **where(last, c)).wait_send()
        across(t, j, bufs[t][j].at[c]).wait_send()

    contract_last = (((1,), (1,)), ((), ()))

    def rows_of(j):
        return pl.ds(starts[j] * 16, sizes[j] * 16)

    def forward(j, lo, hi):
        @pl.loop(lo, hi)
        def _(i):
            cols = pl.ds(pl.multiple_of(i * 256, 256), 256)
            pre[pl.ds(0, sizes[j] * 16), cols] = lax.dot_general(
                xs[j][0], wgu[0, cols, :], contract_last, preferred_element_type=f32
            ) + lax.dot_general(xs[j][1], wgu[1, cols, :], contract_last, preferred_element_type=f32)

    def hidden_backward(j):
        @pl.loop(0, sizes[j] * 16 // 256)
        def _(i):
            at = pl.ds(pl.multiple_of(i * 256, 256), 256)
            hgrad[at, :] = lax.dot_general(
                ds_[j][0, at, pl.ds(0, half)], wd[0], contract_last, preferred_element_type=f32
            ) + lax.dot_general(ds_[j][1, at, pl.ds(0, half)], wd[1], contract_last, preferred_element_type=f32)

        @pl.loop(0, sizes[j] * 16 // 64)
        def _(i):
            there = pl.ds(pl.multiple_of(i * 64, 64), 64)
            here = pl.ds(pl.multiple_of(starts[j] * 16 + i * 64, 64), 64)
            lane = lax.broadcasted_iota(jnp.int32, (64, 128), 1)
            pieces = ds_[j][0, there, pl.ds(half, 128)].astype(f32)
            weight = jnp.sum(jnp.where(jnp.bitwise_and(lane, 15) == e, pieces, 0.0), axis=1, keepdims=True)
            gate_pre, up_pre = pre[there, pl.ds(0, hidden)], pre[there, pl.ds(hidden, hidden)]
            sigmoid = 1.0 / (1.0 + jnp.exp(-gate_pre))
            active = gate_pre * sigmoid
            grad = hgrad[there, :] * weight
            hid[here, :] = (active * up_pre * weight).astype(jnp.bfloat16)
            act[here, pl.ds(hidden, hidden)] = (grad * active).astype(jnp.bfloat16)
            act[here, pl.ds(0, hidden)] = (
                grad * up_pre * sigmoid * (1.0 + gate_pre * (1.0 - sigmoid))).astype(jnp.bfloat16)

    def transposed(j):
        act_t[:, rows_of(j)] = act[rows_of(j), :].T
        hid_t[:, rows_of(j)] = hid[rows_of(j), :].T

    def row_backward(j, side, dest):
        @pl.loop(0, half // 512)
        def _(i):
            cols = pl.ds(pl.multiple_of(i * 512, 512), 512)
            dest[j][:, cols] = jnp.dot(
                act[rows_of(j), :], wgu[side, :, cols], preferred_element_type=f32).astype(jnp.bfloat16)

    def plane_of(q):
        swapped = (0, 1, 3, 2)[q]
        turn = q + ((z + 1) // 2 % 2) * (swapped - q)
        high = z // 2
        return high * turn + (1 - high) * (3 - turn)

    planes = [plane_of(q) for q in range(4)]

    def sibling_copy(j, zz):
        at = pl.ds(pl.multiple_of(zz * 4 * sizes[j], 16), 4 * sizes[j])
        return pltpu.make_async_remote_copy(
            src_ref=sib_out[j].at[at], dst_ref=sib_in[j].at[at], send_sem=sib_send.at[j, zz],
            recv_sem=sib_recv.at[j, zz], **where(e, 1 - c))

    def row_backward_out(j):
        row_backward(j, 1 - c, sib_out)
        for zz in planes:
            sibling_copy(j, zz).start()

    def row_backward_own(j):
        row_backward(j, c, part)

    def add_rows(j, start, count, sources):
        dest = part[j]

        @pl.loop(0, count // 16)
        def _(i):
            here = pl.ds(pl.multiple_of(start + i * 16, 16), 16)
            total = dest[here, :].astype(f32)
            for ref, lead, offset in sources:
                there = pl.ds(pl.multiple_of(offset + i * 16, 16), 16)
                total = total + (ref[there, :] if lead is None else ref[lead, there, :]).astype(f32)
            dest[here, :] = total.astype(jnp.bfloat16)

    def last_copy(j, zz, aa):
        slot = zz * 2 + aa
        return pltpu.make_async_remote_copy(
            src_ref=part[j].at[block(j, index(aa, 1 - b, zz))], dst_ref=from_last[j].at[slot],
            send_sem=last_send.at[j, slot], recv_sem=last_recv.at[j, slot], **where(last, c))

    def z_copy(j, way, zz, aa):
        slot = (zz + 1 - way) * 2 + aa
        return pltpu.make_async_remote_copy(
            src_ref=part[j].at[block(j, index(aa, b, zz))], dst_ref=from_z[j].at[slot],
            send_sem=z_send.at[j, slot], recv_sem=z_recv.at[j, slot], **where(down if way else up, c))

    def reduce_last(j, q):
        zz = planes[q]
        sibling_copy(j, zz).wait_recv()
        for aa in range(2):
            start = index(aa, 1 - b, zz) * sizes[j]
            add_rows(j, start, sizes[j], [(sib_in[j], None, start)])
            last_copy(j, zz, aa).start()

    def reduce_z(j, q):
        zz, final = planes[q], q == 3
        for aa in range(2):
            start = index(aa, b, zz) * sizes[j]
            last_copy(j, zz, aa).wait_recv()
            add_rows(j, start, sizes[j], [(sib_in[j], None, start), (from_last[j], zz * 2 + aa, 0)])
            for way in range(2):
                reached = (z > 0) if way == 0 else (z < 3)
                ours = True if final else (zz > z if way == 0 else zz < z)

                @pl.when(jnp.logical_and(reached, ours))
                def _():
                    z_copy(j, way, zz, aa).wait_recv()
                    add_rows(j, start, sizes[j], [(from_z[j], (zz + 1 - way) * 2 + aa, 0)])

                if not final:
                    pl.when(ours)(z_copy(j, way, zz, aa).start)

    def first_copy(j):
        return pltpu.make_async_remote_copy(
            src_ref=part[j].at[block(j, first)], dst_ref=from_first[j], send_sem=first_send.at[j],
            recv_sem=first_recv.at[j], **where(first, c))

    def finish(j):
        first_copy(j).wait_recv()

        @pl.loop(0, sizes[j] // 16)
        def _(i):
            here = pl.ds(pl.multiple_of(i * 16, 16), 16)
            mine = pl.ds(pl.multiple_of(e * sizes[j] + i * 16, 16), 16)
            out_ref[pl.ds(pl.multiple_of(starts[j] + i * 16, 16), 16), :] = (
                part[j][mine, :].astype(f32) + from_first[j][here, :].astype(f32)).astype(jnp.bfloat16)

    outs = (gg_ref, gu_ref, gd_ref)

    def weight_copy(m, h):
        held = wgu.at[h, pl.ds(m * hidden, hidden)] if m < 2 else wd.at[h]
        return pltpu.make_async_copy(held, outs[m].at[0, :, pl.ds(h * half, half)], out_sem.at[m, h])

    def weight_grad(m, h):
        lhs, rhs = (act_t, xs) if m < 2 else (hid_t, ds_)
        base = m * hidden if m < 2 else 0

        @pl.loop(0, half // 512)
        def _(i):
            cols = pl.ds(pl.multiple_of(i * 512, 512), 512)
            total = jnp.dot(
                lhs[pl.ds(base, hidden), rows_of(0)], rhs[0][h, :, cols], preferred_element_type=f32
            ) + jnp.dot(lhs[pl.ds(base, hidden), rows_of(1)], rhs[1][h, :, cols], preferred_element_type=f32)
            if m < 2:
                wgu[h, pl.ds(base, hidden), cols] = total.astype(jnp.bfloat16)
            else:
                wd[h, :, cols] = total.astype(jnp.bfloat16)

        weight_copy(m, h).start()

    X, G = 0, 1
    own(X, 0)
    first_step(X, 0)
    z_step(X, 0, 1)
    own(G, 0)
    last_step(X, 0, 0)
    z_step(X, 0, 2)
    last_step(X, 0, 1)
    z_step(X, 0, 3)
    first_step(G, 0)
    last_step(X, 0, 2)
    z_step(G, 0, 1)
    last_step(X, 0, 3)
    last_step(G, 0, 0)
    own(X, 1)
    for copy in weights:
        copy.wait()
    z_step(G, 0, 2)
    sibling_step(X, 0)
    forward(0, 0, 1)
    last_step(G, 0, 1)
    z_step(G, 0, 3)
    first_step(X, 1)
    own(G, 1)
    forward(0, 1, 2)
    last_step(G, 0, 2)
    z_step(X, 1, 1)
    forward(0, 2, 3)
    last_step(G, 0, 3)
    last_step(X, 1, 0)
    sibling_step(G, 0)

    hidden_backward(0)
    z_step(X, 1, 2)
    last_step(X, 1, 1)
    first_step(G, 1)
    row_backward_out(0)
    z_step(X, 1, 3)
    last_step(X, 1, 2)
    z_step(G, 1, 1)
    row_backward_own(0)
    last_step(X, 1, 3)
    last_step(G, 1, 0)
    reduce_last(0, 0)
    z_step(G, 1, 2)
    reduce_last(0, 1)
    last_step(G, 1, 1)
    reduce_z(0, 0)
    sibling_step(X, 1)
    z_step(G, 1, 3)
    reduce_last(0, 2)
    reduce_z(0, 1)
    last_step(G, 1, 2)
    reduce_last(0, 3)
    forward(1, 0, 3)
    last_step(G, 1, 3)
    reduce_z(0, 2)
    transposed(0)
    sibling_step(G, 1)

    hidden_backward(1)
    row_backward_out(1)
    row_backward_own(1)
    reduce_z(0, 3)
    first_copy(0).start()
    reduce_last(1, 0)
    reduce_last(1, 1)
    reduce_last(1, 2)
    reduce_z(1, 0)
    reduce_last(1, 3)
    transposed(1)
    weight_grad(0, 0)
    reduce_z(1, 1)
    weight_grad(0, 1)
    reduce_z(1, 2)
    weight_grad(1, 0)
    finish(0)
    reduce_z(1, 3)
    first_copy(1).start()
    weight_grad(1, 1)
    weight_grad(2, 0)
    weight_grad(2, 1)
    finish(1)

    for m in range(3):
        for h in range(2):
            weight_copy(m, h).wait()
    for j in range(2):
        first_copy(j).wait_send()
        for q in range(4):
            zz = planes[q]
            sibling_copy(j, zz).wait_send()
            for aa in range(2):
                last_copy(j, zz, aa).wait_send()
                if q < 3:
                    pl.when(zz > z)(z_copy(j, 0, zz, aa).wait_send)
                    pl.when(zz < z)(z_copy(j, 1, zz, aa).wait_send)
        gather_sent(0, j)
        gather_sent(1, j)


def on_device_tree(tokens, cotangent, expert_ids, gate_values, w_gate, w_up, w_down):
    rows, half = tokens.shape
    hidden = w_gate.shape[1]
    experts = lax.axis_size("expert")
    total = rows * experts
    sizes = (rows // 48 * 32, rows // 48 * 16)
    chosen = expert_ids[:, :, None] == jnp.arange(experts, dtype=jnp.int32)[None, None, :]
    dense = jnp.sum(jnp.where(chosen, gate_values[:, :, None], 0.0), axis=1)
    high = lax.reduce_precision(dense, 8, 7)
    middle = lax.reduce_precision(dense - high, 8, 7)
    low = dense - high - middle
    gates = jnp.concatenate(
        [high, middle, low, jnp.zeros((rows, 128 - 3 * experts), jnp.float32)], axis=1).astype(jnp.bfloat16)
    bf16, f32 = jnp.bfloat16, jnp.float32
    any_, vmem = pl.BlockSpec(memory_space=pl.ANY), pl.BlockSpec(memory_space=pltpu.VMEM)
    dma = pltpu.SemaphoreType.DMA
    whole = tuple(size * experts for size in sizes)

    def chunks(*shape):
        return [pltpu.VMEM(tuple(n[j] if isinstance(n, tuple) else n for n in shape), bf16) for j in range(2)]

    return tuple(pl.pallas_call(
        functools.partial(merge_kernel, sizes),
        out_shape=(
            jax.ShapeDtypeStruct(tokens.shape, bf16),
            jax.ShapeDtypeStruct(w_gate.shape, bf16),
            jax.ShapeDtypeStruct(w_up.shape, bf16),
            jax.ShapeDtypeStruct(w_down.shape, bf16),
        ),
        in_specs=[any_, any_, vmem, any_, any_, any_],
        out_specs=(vmem, any_, any_, any_),
        scratch_shapes=[
            chunks(2, whole, half),
            chunks(2, whole, half + 128),
            pltpu.VMEM((2, 2 * hidden, half), bf16),
            pltpu.VMEM((2, hidden, half), bf16),
            pltpu.VMEM((whole[0], 2 * hidden), f32),
            pltpu.VMEM((whole[0], hidden), f32),
            pltpu.VMEM((total, 2 * hidden), bf16),
            pltpu.VMEM((total, hidden), bf16),
            pltpu.VMEM((2 * hidden, total), bf16),
            pltpu.VMEM((hidden, total), bf16),
            chunks(whole, half),
            chunks(whole, half),
            chunks(whole, half),
            chunks(8, sizes, half),
            chunks(10, sizes, half),
            chunks(sizes, half),
            dma((10,)),
            dma((4, 4, 16)),
            dma((4, 16)),
            dma((4,)),
            dma((4,)),
            dma((2, 4)),
            dma((2, 4)),
            dma((2, 8)),
            dma((2, 8)),
            dma((2, 10)),
            dma((2, 10)),
            dma((2,)),
            dma((2,)),
            dma((3, 2)),
        ],
        compiler_params=pltpu.CompilerParams(
            collective_id=0, has_side_effects=True, vmem_limit_bytes=43 * 1024 * 1024),
        cost_estimate=pl.CostEstimate(
            flops=16 * total * hidden * 2 * half, bytes_accessed=24 * hidden * half, transcendentals=total * hidden),
    )(tokens, cotangent, gates, w_gate, w_up, w_down))


def solution(mesh):
    tree = mesh.shape["expert"] == 16 and mesh.shape["tensor"] == 2
    return jax.shard_map(
        on_device_tree if tree else on_device,
        mesh=mesh,
        in_specs=(
            P("expert", "tensor"),
            P("expert", "tensor"),
            P("expert", None),
            P("expert", None),
            P("expert", "tensor", None),
            P("expert", "tensor", None),
            P("expert", "tensor", None),
        ),
        out_specs=(
            P("expert", "tensor"),
            P("expert", "tensor", None),
            P("expert", "tensor", None),
            P("expert", "tensor", None),
        ),
        check_vma=False,
    )
```
